32 devices in a mesh: bxy: 8 (over z, x), bz: 4 (over y, core).
Axes of the slice: x: 2, y: 2, z: 4, core: 2. Of those that a mesh axis runs over, the one named last changes fastest.
Arguments:
- basis: float32 [48, 245760], P(None, ('bxy', 'bz')), may hold values from -12 to 12
- velocity: float32 [3, 8, 48, 128], P(None, 'bxy'), may hold values from -0.2 to 0.2
- temper: float32 [8, 48, 128], P('bxy'), may hold values from 0.5 to 1.5
- flags: int32 [8, 48, 128], P('bxy'), may hold values 0 or 1
- order: int32 [8, 30720], P('bxy'), may hold values from 0 to 30719, each once within a row
Outputs:
- ortho: float32 [16, 245760], P(None, ('bxy', 'bz'))
- proj: float32 [48, 16], replicated
- upper: float32 [16, 16], replicated
The draws below stay inside these ranges and needn't reach their ends.
Inputs may be any that keep to these rules, and one draw needn't show every extreme that they name: `order`: for each slab, a permutation of its 30720 local rows.
All inputs are finite; a program needn't handle non-finite values. No bound on the sum of `flags` on one device may be relied on, other than what follows from the above.
Results may differ from the reference program's by a relative error of at most 0.0003.
Values sent between devices are 32-bit elements; how exact they have to be, the bound alone decides.
A program may use at most 128 MiB of HBM per device.

```python
import math
import jax
import jax.numpy as jnp
from jax import lax

CX = 1
NZ = 48
CY = 128
BLK = 16
KB = 48
STEPS = 2
NX = 8
SLAB_ROWS = 30720
MROWS = 245760
N_BXY = 8
N_BZ = 4


def draw_basis(key, part):
    first, second = jax.random.split(key, 2)
    levels = jax.random.uniform(second, (1, MROWS), minval=0.0, maxval=math.log(10.0))
    scales = jnp.exp(levels) / 4.6
    raw = jax.random.normal(first, (KB, MROWS))
    return jnp.clip(raw * scales, -12.0, 12.0).astype(jnp.float32)


def set_ends(drawn, own_key, least, largest):
    shape = drawn.shape
    index_at = [jax.random.randint(jax.random.fold_in(own_key, axis), (), 0, shape[axis]) for axis in range(len(shape))]
    drawn = drawn.at[tuple(index_at)].set(least)
    longest = shape.index(max(shape))
    index_at[longest] = (index_at[longest] + 1) % shape[longest]
    return drawn.at[tuple(index_at)].set(largest)


def shard_levels(stream_key, dims, shards, smallest, largest):
    level, own = 1.0, jax.random.fold_in(stream_key, 6)
    for position, shards_of in shards:
        heights = jnp.exp(jax.random.uniform(jax.random.fold_in(own, position), (shards_of,), jnp.float32, smallest / len(shards), largest / len(shards)))
        level = level * jnp.repeat(heights, dims[position] // shards_of).reshape([-1 if axis == position else 1 for axis in range(len(dims))])
    return level


def scatter_about(stream_key, extent, deviation, reach, shards=(), kind=jnp.bfloat16):
    values = deviation * jax.random.normal(stream_key, extent, jnp.float32)
    if shards:
        values = values * shard_levels(stream_key, extent, shards, -0.22, 0.18)
    return jnp.clip(values, -reach, reach).astype(kind)


def setup_inputs(seed: int = 0) -> dict:
    arg_keys = jax.random.split(jax.random.key(seed), 6)
    return {
        "basis": draw_basis(jax.random.fold_in(arg_keys[5], 71), 0),
        "velocity": scatter_about(arg_keys[1], (3, NX, NZ, CY), 0.06, 0.2, ((1, 8),), jnp.float32),
        "temper": jnp.clip(0.5 + 1.0 * jax.random.uniform(arg_keys[2], (NX, NZ, CY), jnp.float32) ** shard_levels(arg_keys[2], (NX, NZ, CY), ((0, 8),), -0.2, 0.2), 0.5, 1.5),
        "flags": set_ends((jax.random.randint(arg_keys[3], (NX, NZ, CY), 0, 12) < 1).astype(jnp.int32), jax.random.fold_in(arg_keys[3], 1), 0, 1),
        "order": jax.vmap(lambda own: jax.random.permutation(own, SLAB_ROWS))(jax.random.split(arg_keys[4], N_BXY)).reshape((N_BXY, SLAB_ROWS)).astype(jnp.int32),
    }


FLOW_DIRS = ((0, 0, 0), (1, 0, 0), (-1, 0, 0), (0, 1, 0), (0, -1, 0), (0, 0, 1), (0, 0, -1), (1, 1, 0), (-1, -1, 0), (1, -1, 0), (-1, 1, 0), (1, 0, 1), (-1, 0, -1), (1, 0, -1), (-1, 0, 1), (0, 1, 1), (0, -1, -1), (0, 1, -1), (0, -1, 1))
FLOW_WEIGHTS = (1.0 / 3.0,) + (1.0 / 18.0,) * 6 + (1.0 / 36.0,) * 12
HEAT_WEIGHTS = (0.25,) + (0.125,) * 6
OPPOSITE = (0,) + tuple((number + 1 if number % 2 == 1 else number - 1 for number in range(1, 19)))
OMEGA_FLOW = 1.6
OMEGA_HEAT = 1.4
BUOYANCY = 0.2

def along(direction, comps):
    total = 0.0
    for weight, array in zip(direction, comps):
        if weight == 1:
            total = total + array
        elif weight == -1:
            total = total - array
    return total

def moments(flow, heat):
    density = flow[0]
    for number in range(1, 19):
        density = density + flow[number]
    momentum = []
    for comp in range(3):
        momentum.append(along([FLOW_DIRS[number][comp] for number in range(19)], flow))
    warmth = heat[0]
    for number in range(1, 7):
        warmth = warmth + heat[number]
    return (density, momentum, warmth)

def equilibria(density, momentum, warmth, velocity, temper):
    carried = [momentum[comp] - velocity[comp] * density for comp in range(3)]
    speed_sq = velocity[0] * velocity[0] + velocity[1] * velocity[1] + velocity[2] * velocity[2]
    carried_u = velocity[0] * carried[0] + velocity[1] * carried[1] + velocity[2] * carried[2]
    flow_eq = []
    heat_eq = []
    for number in range(19):
        drift = along(FLOW_DIRS[number], velocity)
        push = along(FLOW_DIRS[number], carried)
        value = density * (1.0 + 3.0 * drift + 4.5 * drift * drift - 1.5 * speed_sq) + 3.0 * push + 9.0 * drift * push - 3.0 * carried_u
        flow_eq.append(FLOW_WEIGHTS[number] * value)
        if number < 7:
            heat_eq.append(HEAT_WEIGHTS[number] * (warmth * (1.0 + 4.0 * drift) + 4.0 * temper * push))
    return (flow_eq, heat_eq)

def collide(flow, heat, velocity, temper, solid):
    density, momentum, warmth = moments(flow, heat)
    flow_eq, heat_eq = equilibria(density, momentum, warmth, velocity, temper)
    flow_new = []
    heat_new = []
    for number in range(19):
        fresh = flow[number] - OMEGA_FLOW * (flow[number] - flow_eq[number]) + 3.0 * FLOW_WEIGHTS[number] * FLOW_DIRS[number][1] * BUOYANCY * warmth
        flow_new.append(jnp.where(solid, flow[OPPOSITE[number]], fresh))
    for number in range(7):
        fresh = heat[number] - OMEGA_HEAT * (heat[number] - heat_eq[number])
        heat_new.append(jnp.where(solid, heat[OPPOSITE[number]], fresh))
    return (flow_new, heat_new)

def reference(basis, velocity, temper, flags, order):
    devices = N_BXY * N_BZ
    piece_rows = SLAB_ROWS // devices
    slab_order = order.astype(jnp.int32)
    counter = jnp.arange(SLAB_ROWS, dtype=jnp.int32)
    inverse = jax.vmap(lambda row: jnp.zeros((SLAB_ROWS,), jnp.int32).at[row].set(counter))(slab_order)
    block = basis[KB - BLK:]
    permuted = block.reshape(BLK, devices, N_BXY, piece_rows).transpose(0, 2, 1, 3).reshape(BLK, N_BXY, SLAB_ROWS)
    slabs = jnp.take_along_axis(permuted, jnp.broadcast_to(inverse[None], permuted.shape), axis=2)
    fields = slabs.reshape(BLK, N_BXY, 5, CX, NZ, CY).transpose(0, 2, 1, 3, 4, 5).reshape(BLK, 5, NX, NZ, CY)
    height = lax.broadcasted_iota(jnp.int32, (NX, NZ, CY), 1)
    solid = (flags == 1) | (height == 0) | (height == NZ - 1)
    speeds = [velocity[0], velocity[1], velocity[2]]

    def evolve(field):
        flow, heat = equilibria(field[0], [field[1], field[2], field[3]], field[4], speeds, temper)
        for turn in range(STEPS):
            flow, heat = collide(flow, heat, speeds, temper, solid)
            flow = [jnp.roll(flow[number], FLOW_DIRS[number], axis=(0, 1, 2)) for number in range(19)]
            heat = [jnp.roll(heat[number], FLOW_DIRS[number], axis=(0, 1, 2)) for number in range(7)]
        density, momentum, warmth = moments(flow, heat)
        return jnp.stack([density] + momentum + [warmth], 0)
    evolved = lax.map(evolve, fields)
    back = evolved.reshape(BLK, 5, N_BXY, CX, NZ, CY).transpose(0, 2, 1, 3, 4, 5).reshape(BLK, N_BXY, SLAB_ROWS)
    reordered = jnp.take_along_axis(back, jnp.broadcast_to(slab_order[None], back.shape), axis=2)
    work = reordered.reshape(BLK, N_BXY, devices, piece_rows).transpose(0, 2, 1, 3).reshape(BLK, MROWS)
    highest = lax.Precision.HIGHEST
    proj = jnp.dot(basis, work.T, precision=highest) / MROWS
    resid = work - jnp.dot(proj.T, basis, precision=highest)
    gram = jnp.dot(resid, resid.T, precision=highest) / MROWS
    lower = jnp.linalg.cholesky(gram)
    ortho = lax.linalg.triangular_solve(lower, resid, left_side=True, lower=True)
    return (ortho, proj, lower.T)
```

```python
import functools

import jax
import jax.numpy as jnp
from jax import lax
from jax.experimental import pallas as pl
from jax.experimental.pallas import tpu as pltpu
from jax.sharding import PartitionSpec as P

BLK = 16
KB = 48
CORES = 2
LANES = 128
VMEM_BYTES = 56 * 1024 * 1024


FLOW_DIRS = (
    (0, 0, 0),
    (1, 0, 0),
    (-1, 0, 0),
    (0, 1, 0),
    (0, -1, 0),
    (0, 0, 1),
    (0, 0, -1),
    (1, 1, 0),
    (-1, -1, 0),
    (1, -1, 0),
    (-1, 1, 0),
    (1, 0, 1),
    (-1, 0, -1),
    (1, 0, -1),
    (-1, 0, 1),
    (0, 1, 1),
    (0, -1, -1),
    (0, 1, -1),
    (0, -1, 1),
)
ALL_DIRS = FLOW_DIRS + FLOW_DIRS[:7]
FLOW_WEIGHTS = (1.0 / 3.0,) + (1.0 / 18.0,) * 6 + (1.0 / 36.0,) * 12
HEAT_WEIGHTS = (0.25,) + (0.125,) * 6
OPPOSITE = (0,) + tuple((number + 1 if number % 2 == 1 else number - 1 for number in range(1, 19)))
OMEGA_FLOW = 1.6
OMEGA_HEAT = 1.4
BUOYANCY = 0.2


def along(direction, comps):
    total = None
    for weight, array in zip(direction, comps):
        if weight == 1:
            total = array if total is None else total + array
        elif weight == -1:
            total = -array if total is None else total - array
    return total


def moments(flow, heat):
    density = flow[0]
    for number in range(1, 19):
        density = density + flow[number]
    momentum = []
    for comp in range(3):
        momentum.append(along([FLOW_DIRS[number][comp] for number in range(19)], flow))
    warmth = heat[0]
    for number in range(1, 7):
        warmth = warmth + heat[number]
    return (density, momentum, warmth)


def equilibria(density, momentum, warmth, velocity, temper):
    carried = [momentum[comp] - velocity[comp] * density for comp in range(3)]
    speed_sq = velocity[0] * velocity[0] + velocity[1] * velocity[1] + velocity[2] * velocity[2]
    carried_u = velocity[0] * carried[0] + velocity[1] * carried[1] + velocity[2] * carried[2]
    rest = density * (1.0 - 1.5 * speed_sq) - 3.0 * carried_u
    flow_eq = [FLOW_WEIGHTS[0] * rest] + [None] * 18
    heat_eq = [HEAT_WEIGHTS[0] * warmth] + [None] * 6
    for number in range(1, 19, 2):
        drift = along(FLOW_DIRS[number], velocity)
        push = along(FLOW_DIRS[number], carried)
        even = rest + drift * (4.5 * drift * density + 9.0 * push)
        odd = 3.0 * (drift * density + push)
        flow_eq[number] = FLOW_WEIGHTS[number] * (even + odd)
        flow_eq[number + 1] = FLOW_WEIGHTS[number] * (even - odd)
        if number < 7:
            tilt = 4.0 * (warmth * drift + temper * push)
            heat_eq[number] = HEAT_WEIGHTS[number] * (warmth + tilt)
            heat_eq[number + 1] = HEAT_WEIGHTS[number] * (warmth - tilt)
    return (flow_eq, heat_eq)


def lattice_kernel(count, high, fields_ref, base_ref, out_ref, first_ref, second_ref):
    wide = fields_ref.shape[2]

    def base_at(x):
        return (
            [base_ref[x, 0], base_ref[x, 1], base_ref[x, 2]],
            base_ref[x, 3],
            base_ref[x, 4] > 0.5,
        )

    def force(number, warmth):
        return 3.0 * FLOW_WEIGHTS[number] * FLOW_DIRS[number][1] * BUOYANCY * warmth

    def streamed(ref, x):
        found = []
        for number in range(26):
            first, second, third = ALL_DIRS[number]
            value = ref[number, lax.rem(x + count - first, count)]
            if second:
                value = pltpu.roll(value, second % wide, 0)
            if third:
                value = pltpu.roll(value, third % LANES, 1)
            found.append(value)
        return (found[:19], found[19:])

    def begin(x, carry):
        velocity, temper, solid = base_at(x)
        warmth = fields_ref[x, 4]
        flow, heat = equilibria(
            fields_ref[x, 0],
            [fields_ref[x, 1], fields_ref[x, 2], fields_ref[x, 3]],
            warmth,
            velocity,
            temper,
        )
        for number in range(19):
            fresh = flow[number]
            if FLOW_DIRS[number][1]:
                fresh = fresh + force(number, warmth)
            first_ref[number, x] = jnp.where(solid, flow[OPPOSITE[number]], fresh)
        for number in range(7):
            first_ref[19 + number, x] = jnp.where(solid, heat[OPPOSITE[number]], heat[number])
        return carry

    def again(x, carry):
        velocity, temper, solid = base_at(x)
        flow, heat = streamed(first_ref, x)
        density, momentum, warmth = moments(flow, heat)
        flow_eq, heat_eq = equilibria(density, momentum, warmth, velocity, temper)
        for number in range(19):
            fresh = (1.0 - OMEGA_FLOW) * flow[number] + OMEGA_FLOW * flow_eq[number]
            if FLOW_DIRS[number][1]:
                fresh = fresh + force(number, warmth)
            second_ref[number, x] = jnp.where(solid, flow[OPPOSITE[number]], fresh)
        for number in range(7):
            fresh = (1.0 - OMEGA_HEAT) * heat[number] + OMEGA_HEAT * heat_eq[number]
            second_ref[19 + number, x] = jnp.where(solid, heat[OPPOSITE[number]], fresh)
        return carry

    def finish(x, carry):
        flow, heat = streamed(second_ref, x)
        density, momentum, warmth = moments(flow, heat)
        for number, value in enumerate([density] + momentum + [warmth]):
            out_ref[x, number] = value[2 : 2 + high]
        return carry

    lax.fori_loop(0, count, begin, 0)
    lax.fori_loop(0, count, again, 0)
    lax.fori_loop(0, count, finish, 0)


def spread_kernel(piece, tall, order_ref, arrived_ref, mine_ref, other_ref, rows_ref, spread_ref):
    core = lax.rem(lax.axis_index("bz"), CORES)
    panels, vecs, padded = arrived_ref.shape
    step = 16 if piece % 16 == 0 else 8
    wide = mine_ref.shape[2]
    half = tall // CORES
    total = spread_ref.shape[0]

    def clear(i, carry):
        spread_ref[pl.ds(pl.multiple_of(i * 256, 256), 256), :] = jnp.zeros((256, LANES), jnp.float32)
        return carry

    lax.fori_loop(0, total // 256, clear, 0)

    def panel(i, carry):
        for start in range(0, padded, LANES):
            rows_ref[start : start + LANES, 0:vecs] = arrived_ref[i, :, start : start + LANES].T
        base = (CORES * i + core) * piece

        def rows(j, carry):
            at = pl.multiple_of(j * step, step)
            held = [rows_ref[pl.ds(at + t, 1), :] for t in range(step)]
            where = [order_ref[0, base + at + t] for t in range(step)]
            for t in range(step):
                spread_ref[pl.ds(where[t], 1), :] = held[t]
            return carry

        return lax.fori_loop(0, piece // step, rows, carry)

    lax.fori_loop(0, panels, panel, 0)

    for out_ref, which in ((mine_ref, core), (other_ref, 1 - core)):

        def moment(m, carry):
            for r in range(wide):
                level = lax.rem(half * which + tall - 2 + r, tall)
                start = pl.multiple_of((m * tall + level) * LANES, LANES)
                block = spread_ref[pl.ds(start, LANES), :].T
                for v in range(vecs):
                    out_ref[v, m, r : r + 1, :] = block[v : v + 1, :]
            return carry

        lax.fori_loop(0, 5, moment, 0)


def collect_kernel(piece, tall, order_ref, mine_ref, other_ref, out_ref, rows_ref, table_ref):
    core = lax.rem(lax.axis_index("bz"), CORES)
    panels, vecs, padded = out_ref.shape
    step = 16 if piece % 16 == 0 else 8
    half = tall // CORES

    for in_ref, which in ((mine_ref, core), (other_ref, 1 - core)):

        def moment(m, carry):
            for r in range(half):
                start = pl.multiple_of((m * tall + half * which + r) * LANES, LANES)
                block = jnp.concatenate([in_ref[v, m, r : r + 1, :] for v in range(vecs)], 0)
                table_ref[pl.ds(start, LANES), 0:vecs] = block.T
            return carry

        lax.fori_loop(0, 5, moment, 0)

    def panel(i, carry):
        base = (CORES * i + core) * piece

        def rows(j, carry):
            at = pl.multiple_of(j * step, step)
            where = [order_ref[0, base + at + t] for t in range(step)]
            held = [table_ref[pl.ds(where[t], 1), :] for t in range(step)]
            for t in range(step):
                rows_ref[pl.ds(at + t, 1), :] = held[t]
            return carry

        lax.fori_loop(0, piece // step, rows, 0)
        for start in range(0, padded, LANES):
            block = rows_ref[start : start + LANES, :].T
            out_ref[i, :, start : start + LANES] = block[0:vecs, :]
        return carry

    lax.fori_loop(0, panels, panel, 0)


def vmem():
    return pl.BlockSpec(memory_space=pltpu.VMEM)


def smem():
    return pl.BlockSpec(memory_space=pltpu.SMEM)


def params():
    return pltpu.CompilerParams(vmem_limit_bytes=VMEM_BYTES)


def swap_cores(array):
    count = lax.axis_size("bz")
    return lax.ppermute(array, "bz", [(i, i ^ 1) for i in range(count)])


def exchange(array):
    pairs = [[c + CORES * k for k in range(lax.axis_size("bz") // CORES)] for c in range(CORES)]
    array = lax.all_to_all(array, "bxy", split_axis=0, concat_axis=0, tiled=True)
    return lax.all_to_all(
        array, "bz", split_axis=1, concat_axis=1, tiled=True, axis_index_groups=pairs
    )


def body(basis, velocity, temper, flags, order):
    count_first = lax.axis_size("bxy")
    count_second = lax.axis_size("bz")
    devices = count_first * count_second
    panel_rows = basis.shape[1]
    piece = panel_rows // count_first
    slab_rows = piece * devices
    total_rows = panel_rows * devices
    tall, third = temper.shape[1:]
    ways = count_second // CORES
    vecs = BLK // ways
    parts = count_first // vecs
    high = tall // CORES // parts
    wide = -(-(tall // CORES + 4) // 8) * 8
    piece_wide = -(-(high + 4) // 8) * 8
    padded = -(-piece // LANES) * LANES
    panels = devices // CORES
    me_first = lax.axis_index("bxy")
    core = lax.rem(lax.axis_index("bz"), CORES)

    height = lax.broadcasted_iota(jnp.int32, temper.shape, 1)
    solid = (flags == 1) | (height == 0) | (height == tall - 1)
    base = jnp.concatenate([velocity, temper[None], solid.astype(jnp.float32)[None]], 0)
    base = base.transpose(1, 0, 2, 3)
    ring = jnp.concatenate([base[:, :, tall - 2 :], base, base[:, :, : wide]], 2)
    ring = lax.dynamic_slice_in_dim(ring, core * (tall // CORES), wide, 2)
    ring = lax.all_gather(ring, "bxy", axis=0, tiled=True)
    part = me_first // vecs
    if parts > 1:
        ring = jnp.concatenate([ring, ring[:, :, :8]], 2)
        ring = lax.dynamic_slice_in_dim(ring, part * high, piece_wide, 2)

    outgoing = basis[KB - BLK :].reshape(ways, vecs, count_first, piece).transpose(2, 0, 1, 3)
    outgoing = jnp.pad(outgoing, ((0, 0), (0, 0), (0, 0), (0, padded - piece)))
    arrived = exchange(outgoing).reshape(panels, vecs, padded)
    part_shape = jax.ShapeDtypeStruct((vecs, 5, wide, third), jnp.float32)
    mine, other = pl.pallas_call(
        functools.partial(spread_kernel, piece, tall),
        out_shape=(part_shape, part_shape),
        in_specs=[smem(), vmem()],
        out_specs=(vmem(), vmem()),
        scratch_shapes=[
            pltpu.VMEM((padded, LANES), jnp.float32),
            pltpu.VMEM((slab_rows, LANES), jnp.float32),
        ],
        compiler_params=params(),
    )(order, arrived)
    whole = mine + swap_cores(other)
    if parts > 1:
        whole = jnp.pad(whole, ((0, 0), (0, 0), (0, 8), (0, 0)))
        whole = jnp.concatenate(
            [whole[:, :, s * high : s * high + piece_wide] for s in range(parts)], 0
        )
    fields = lax.all_to_all(whole, "bxy", split_axis=0, concat_axis=0, tiled=True)

    state = pltpu.VMEM((26, count_first, piece_wide, third), jnp.float32)
    evolved = pl.pallas_call(
        functools.partial(lattice_kernel, count_first, high),
        out_shape=jax.ShapeDtypeStruct((count_first, 5, high, third), jnp.float32),
        in_specs=[vmem(), vmem()],
        out_specs=vmem(),
        scratch_shapes=[state, state],
        compiler_params=params(),
    )(fields, ring)

    back = lax.all_to_all(evolved, "bxy", split_axis=0, concat_axis=0, tiled=True)
    if parts > 1:
        back = (
            back.reshape(parts, vecs, 5, high, third)
            .transpose(1, 2, 0, 3, 4)
            .reshape(vecs, 5, parts * high, third)
        )
    leaving = pl.pallas_call(
        functools.partial(collect_kernel, piece, tall),
        out_shape=jax.ShapeDtypeStruct((panels, vecs, padded), jnp.float32),
        in_specs=[smem(), vmem(), vmem()],
        out_specs=vmem(),
        scratch_shapes=[
            pltpu.VMEM((padded, LANES), jnp.float32),
            pltpu.VMEM((slab_rows, LANES), jnp.float32),
        ],
        compiler_params=params(),
    )(order, back, swap_cores(back))
    landed = exchange(leaving.reshape(count_first, ways, vecs, padded))
    work = landed[..., :piece].transpose(1, 2, 0, 3).reshape(BLK, panel_rows)

    highest = lax.Precision.HIGHEST
    proj = lax.psum(jnp.dot(basis, work.T, precision=highest), ("bxy", "bz")) / total_rows
    resid = work - jnp.dot(proj.T, basis, precision=highest)
    gram = lax.psum(jnp.dot(resid, resid.T, precision=highest), ("bxy", "bz")) / total_rows
    lower = jnp.linalg.cholesky(gram)
    ortho = lax.linalg.triangular_solve(lower, resid, left_side=True, lower=True)
    return (ortho, proj, lower.T)


def solution(mesh):
    in_specs = (
        P(None, ("bxy", "bz")),
        P(None, "bxy", None, None),
        P("bxy", None, None),
        P("bxy", None, None),
        P("bxy", None),
    )
    out_specs = (P(None, ("bxy", "bz")), P(), P())
    return jax.shard_map(body, mesh=mesh, in_specs=in_specs, out_specs=out_specs, check_vma=False)
```

```python
import functools

import jax
import jax.numpy as jnp
from jax import lax
from jax.experimental import pallas as pl
from jax.experimental.pallas import tpu as pltpu
from jax.sharding import PartitionSpec as P

BLK = 16
KB = 48
CORES = 2
LANES = 128
VMEM_BYTES = 56 * 1024 * 1024


FLOW_DIRS = (
    (0, 0, 0),
    (1, 0, 0),
    (-1, 0, 0),
    (0, 1, 0),
    (0, -1, 0),
    (0, 0, 1),
    (0, 0, -1),
    (1, 1, 0),
    (-1, -1, 0),
    (1, -1, 0),
    (-1, 1, 0),
    (1, 0, 1),
    (-1, 0, -1),
    (1, 0, -1),
    (-1, 0, 1),
    (0, 1, 1),
    (0, -1, -1),
    (0, 1, -1),
    (0, -1, 1),
)
ALL_DIRS = FLOW_DIRS + FLOW_DIRS[:7]
FLOW_WEIGHTS = (1.0 / 3.0,) + (1.0 / 18.0,) * 6 + (1.0 / 36.0,) * 12
HEAT_WEIGHTS = (0.25,) + (0.125,) * 6
OPPOSITE = (0,) + tuple((number + 1 if number % 2 == 1 else number - 1 for number in range(1, 19)))
OMEGA_FLOW = 1.6
OMEGA_HEAT = 1.4
BUOYANCY = 0.2


def along(direction, comps):
    total = None
    for weight, array in zip(direction, comps):
        if weight == 1:
            total = array if total is None else total + array
        elif weight == -1:
            total = -array if total is None else total - array
    return total


def moments(flow, heat):
    density = flow[0]
    for number in range(1, 19):
        density = density + flow[number]
    momentum = []
    for comp in range(3):
        momentum.append(along([FLOW_DIRS[number][comp] for number in range(19)], flow))
    warmth = heat[0]
    for number in range(1, 7):
        warmth = warmth + heat[number]
    return (density, momentum, warmth)


def equilibria(density, momentum, warmth, velocity, temper):
    carried = [momentum[comp] - velocity[comp] * density for comp in range(3)]
    speed_sq = velocity[0] * velocity[0] + velocity[1] * velocity[1] + velocity[2] * velocity[2]
    carried_u = velocity[0] * carried[0] + velocity[1] * carried[1] + velocity[2] * carried[2]
    rest = density * (1.0 - 1.5 * speed_sq) - 3.0 * carried_u
    flow_eq = [FLOW_WEIGHTS[0] * rest] + [None] * 18
    heat_eq = [HEAT_WEIGHTS[0] * warmth] + [None] * 6
    for number in range(1, 19, 2):
        drift = along(FLOW_DIRS[number], velocity)
        push = along(FLOW_DIRS[number], carried)
        even = rest + drift * (4.5 * drift * density + 9.0 * push)
        odd = 3.0 * (drift * density + push)
        flow_eq[number] = FLOW_WEIGHTS[number] * (even + odd)
        flow_eq[number + 1] = FLOW_WEIGHTS[number] * (even - odd)
        if number < 7:
            tilt = 4.0 * (warmth * drift + temper * push)
            heat_eq[number] = HEAT_WEIGHTS[number] * (warmth + tilt)
            heat_eq[number + 1] = HEAT_WEIGHTS[number] * (warmth - tilt)
    return (flow_eq, heat_eq)


def lattice_kernel(count, high, fields_ref, base_ref, out_ref, first_ref, second_ref):
    wide = fields_ref.shape[2]

    def base_at(x):
        return (
            [base_ref[x, 0], base_ref[x, 1], base_ref[x, 2]],
            base_ref[x, 3],
            base_ref[x, 4] > 0.5,
        )

    def force(number, warmth):
        return 3.0 * FLOW_WEIGHTS[number] * FLOW_DIRS[number][1] * BUOYANCY * warmth

    def streamed(ref, x):
        found = []
        for number in range(26):
            first, second, third = ALL_DIRS[number]
            value = ref[number, lax.rem(x + count - first, count)]
            if second:
                value = pltpu.roll(value, second % wide, 0)
            if third:
                value = pltpu.roll(value, third % LANES, 1)
            found.append(value)
        return (found[:19], found[19:])

    def begin(x, carry):
        velocity, temper, solid = base_at(x)
        warmth = fields_ref[x, 4]
        flow, heat = equilibria(
            fields_ref[x, 0],
            [fields_ref[x, 1], fields_ref[x, 2], fields_ref[x, 3]],
            warmth,
            velocity,
            temper,
        )
        for number in range(19):
            fresh = flow[number]
            if FLOW_DIRS[number][1]:
                fresh = fresh + force(number, warmth)
            first_ref[number, x] = jnp.where(solid, flow[OPPOSITE[number]], fresh)
        for number in range(7):
            first_ref[19 + number, x] = jnp.where(solid, heat[OPPOSITE[number]], heat[number])
        return carry

    def again(x, carry):
        velocity, temper, solid = base_at(x)
        flow, heat = streamed(first_ref, x)
        density, momentum, warmth = moments(flow, heat)
        flow_eq, heat_eq = equilibria(density, momentum, warmth, velocity, temper)
        for number in range(19):
            fresh = (1.0 - OMEGA_FLOW) * flow[number] + OMEGA_FLOW * flow_eq[number]
            if FLOW_DIRS[number][1]:
                fresh = fresh + force(number, warmth)
            second_ref[number, x] = jnp.where(solid, flow[OPPOSITE[number]], fresh)
        for number in range(7):
            fresh = (1.0 - OMEGA_HEAT) * heat[number] + OMEGA_HEAT * heat_eq[number]
            second_ref[19 + number, x] = jnp.where(solid, heat[OPPOSITE[number]], fresh)
        return carry

    def finish(x, carry):
        flow, heat = streamed(second_ref, x)
        density, momentum, warmth = moments(flow, heat)
        for number, value in enumerate([density] + momentum + [warmth]):
            out_ref[x, number] = value[2 : 2 + high]
        return carry

    lax.fori_loop(0, count, begin, 0)
    lax.fori_loop(0, count, again, 0)
    lax.fori_loop(0, count, finish, 0)


def spread_kernel(piece, tall, order_ref, arrived_ref, mine_ref, other_ref, rows_ref, spread_ref):
    core = lax.rem(lax.axis_index("bz"), CORES)
    panels, vecs, padded = arrived_ref.shape
    step = 16 if piece % 16 == 0 else 8
    wide = mine_ref.shape[2]
    half = tall // CORES
    total = spread_ref.shape[0]

    def clear(i, carry):
        spread_ref[pl.ds(pl.multiple_of(i * 256, 256), 256), :] = jnp.zeros((256, LANES), jnp.float32)
        return carry

    lax.fori_loop(0, total // 256, clear, 0)

    def panel(i, carry):
        for start in range(0, padded, LANES):
            rows_ref[start : start + LANES, 0:vecs] = arrived_ref[i, :, start : start + LANES].T
        base = (CORES * i + core) * piece

        def rows(j, carry):
            at = pl.multiple_of(j * step, step)
            held = [rows_ref[pl.ds(at + t, 1), :] for t in range(step)]
            where = [order_ref[0, base + at + t] for t in range(step)]
            for t in range(step):
                spread_ref[pl.ds(where[t], 1), :] = held[t]
            return carry

        return lax.fori_loop(0, piece // step, rows, carry)

    lax.fori_loop(0, panels, panel, 0)

    for out_ref, which in ((mine_ref, core), (other_ref, 1 - core)):

        def moment(m, carry):
            for r in range(wide):
                level = lax.rem(half * which + tall - 2 + r, tall)
                start = pl.multiple_of((m * tall + level) * LANES, LANES)
                block = spread_ref[pl.ds(start, LANES), :].T
                for v in range(vecs):
                    out_ref[v, m, r : r + 1, :] = block[v : v + 1, :]
            return carry

        lax.fori_loop(0, 5, moment, 0)


def collect_kernel(piece, tall, order_ref, mine_ref, other_ref, out_ref, rows_ref, table_ref):
    core = lax.rem(lax.axis_index("bz"), CORES)
    panels, vecs, padded = out_ref.shape
    step = 16 if piece % 16 == 0 else 8
    half = tall // CORES

    for in_ref, which in ((mine_ref, core), (other_ref, 1 - core)):

        def moment(m, carry):
            for r in range(half):
                start = pl.multiple_of((m * tall + half * which + r) * LANES, LANES)
                block = jnp.concatenate([in_ref[v, m, r : r + 1, :] for v in range(vecs)], 0)
                table_ref[pl.ds(start, LANES), 0:vecs] = block.T
            return carry

        lax.fori_loop(0, 5, moment, 0)

    def panel(i, carry):
        base = (CORES * i + core) * piece

        def rows(j, carry):
            at = pl.multiple_of(j * step, step)
            where = [order_ref[0, base + at + t] for t in range(step)]
            held = [table_ref[pl.ds(where[t], 1), :] for t in range(step)]
            for t in range(step):
                rows_ref[pl.ds(at + t, 1), :] = held[t]
            return carry

        lax.fori_loop(0, piece // step, rows, 0)
        for start in range(0, padded, LANES):
            block = rows_ref[start : start + LANES, :].T
            out_ref[i, :, start : start + LANES] = block[0:vecs, :]
        return carry

    lax.fori_loop(0, panels, panel, 0)


def exchange_start(send, out_ref, sends, recvs, me, count, place):
    def start(d, carry):
        to = lax.rem(me + d, count)
        remote(send.at[to], out_ref.at[me], sends.at[to], recvs.at[me], place(to)).start()
        return carry

    lax.fori_loop(1, count, start, 0)


def exchange_wait(send, out_ref, sends, recvs, me, count, place, then=None):
    def wait(d, carry):
        source = lax.rem(me + count - d, count)
        remote(send.at[source], out_ref.at[source], sends.at[source], recvs.at[source], place(source)).wait_recv()
        if then is not None:
            then(source)
        return carry

    lax.fori_loop(1, count, wait, 0)


def exchange_drain(send, out_ref, sends, recvs, me, count, place):
    def drain(d, carry):
        to = lax.rem(me + d, count)
        remote(send.at[to], out_ref.at[me], sends.at[to], recvs.at[me], place(to)).wait_send()
        return carry

    lax.fori_loop(1, count, drain, 0)


def remote(source, target, send, recv, place):
    return pltpu.make_async_remote_copy(
        src_ref=source,
        dst_ref=target,
        send_sem=send,
        recv_sem=recv,
        device_id=place,
        device_id_type=pl.DeviceIdType.MESH,
    )


def greet(me, count, place):
    barrier = pltpu.get_barrier_semaphore()

    def hello(d, carry):
        pl.semaphore_signal(
            barrier, inc=1, device_id=place(lax.rem(me + d, count)), device_id_type=pl.DeviceIdType.MESH
        )
        return carry

    lax.fori_loop(1, count, hello, 0)


def position():
    first, second = lax.axis_index("bxy"), lax.axis_index("bz")
    return (first, second, lax.rem(second, CORES), second // CORES)


def panels_kernel(ways, outgoing_ref, arrived_ref, sends, recvs):
    first, _, core, way = position()
    count = outgoing_ref.shape[0]
    me = first * ways + way

    def place(i):
        return (i // ways, lax.rem(i, ways) * CORES + core)

    greet(me, count, place)
    pl.semaphore_wait(pltpu.get_barrier_semaphore(), count - 1)
    group = (outgoing_ref, arrived_ref, sends, recvs, me, count, place)
    exchange_start(*group)
    arrived_ref[me] = outgoing_ref[me]
    exchange_wait(*group)
    exchange_drain(*group)


def gather_kernel(mine_ref, other_ref, out_ref, got_ref, mix_ref, swap_s, swap_r, sends, recvs):
    me, second, core, _ = position()
    count = mine_ref.shape[0]
    sibling = (me, second + 1 - 2 * core)

    def place(i):
        return (i, second)

    greet(me, count, place)
    barrier = pltpu.get_barrier_semaphore()
    pl.semaphore_signal(barrier, inc=1, device_id=sibling, device_id_type=pl.DeviceIdType.MESH)
    pl.semaphore_wait(barrier, count)

    def swap(i):
        return remote(other_ref.at[i], got_ref.at[i], swap_s.at[i], swap_r.at[i], sibling)

    def begin(d, carry):
        swap(lax.rem(me + d, count)).start()
        return carry

    lax.fori_loop(1, count + 1, begin, 0)

    def send(d, carry):
        to = lax.rem(me + d, count)
        swap(to).wait_recv()
        mix_ref[to] = mine_ref[to] + got_ref[to]
        remote(mix_ref.at[to], out_ref.at[me], sends.at[to], recvs.at[me], place(to)).start()
        return carry

    lax.fori_loop(1, count, send, 0)
    swap(me).wait_recv()
    out_ref[me] = mine_ref[me] + got_ref[me]
    group = (mix_ref, out_ref, sends, recvs, me, count, place)
    exchange_wait(*group)
    exchange_drain(*group)

    def end(i, carry):
        swap(i).wait_send()
        return carry

    lax.fori_loop(0, count, end, 0)


def scatter_kernel(evolved_ref, mine_ref, other_ref, swap_s, swap_r, sends, recvs):
    me, second, core, _ = position()
    count = evolved_ref.shape[0]
    sibling = (me, second + 1 - 2 * core)

    def place(i):
        return (i, second)

    greet(me, count, place)
    barrier = pltpu.get_barrier_semaphore()
    pl.semaphore_signal(barrier, inc=1, device_id=sibling, device_id_type=pl.DeviceIdType.MESH)
    pl.semaphore_wait(barrier, count)

    def swap(i):
        return remote(mine_ref.at[i], other_ref.at[i], swap_s.at[i], swap_r.at[i], sibling)

    group = (evolved_ref, mine_ref, sends, recvs, me, count, place)
    exchange_start(*group)
    mine_ref[me] = evolved_ref[me]
    swap(me).start()
    exchange_wait(*group, then=lambda source: swap(source).start())
    exchange_drain(*group)

    def end(i, carry):
        swap(i).wait()
        return carry

    lax.fori_loop(0, count, end, 0)


def project_kernel(
    ways, piece, total_rows, leaving_ref, basis_ref, ortho_ref, proj_ref, upper_ref,
    landed_ref, stack_ref, near_ref, far_ref, sends, recvs, near_s, near_r, far_s, far_r,
):
    first, second, core, way = position()
    count = leaving_ref.shape[0]
    count_second, count_first = near_ref.shape[0], far_ref.shape[0]
    vecs = BLK // ways
    me = first * ways + way

    def place(i):
        return (i // ways, lax.rem(i, ways) * CORES + core)

    greet(me, count, place)
    barrier = pltpu.get_barrier_semaphore()
    for k in range(ways):
        pl.semaphore_signal(
            barrier, inc=1, device_id=(first, k * CORES + 1 - core), device_id_type=pl.DeviceIdType.MESH
        )
    pl.semaphore_wait(barrier, count - 1 + ways)
    group = (leaving_ref, landed_ref, sends, recvs, me, count, place)
    exchange_start(*group)
    landed_ref[me] = leaving_ref[me]
    stack_ref[0:KB] = basis_ref[...]
    exchange_wait(*group)
    for p in range(count_first):
        for k in range(ways):
            stack_ref[KB + k * vecs : KB + (k + 1) * vecs, p * piece : (p + 1) * piece] = landed_ref[
                p * ways + k, :, 0:piece
            ]
    highest = lax.Precision.HIGHEST
    across = (((1,), (1,)), ((), ()))
    stack = stack_ref[...]
    inner = lax.dot_general(stack, stack, across, precision=highest, preferred_element_type=jnp.float32)

    near_ref[second] = jnp.concatenate([inner[0:32], inner[32:64]], 1)
    group_near = (near_ref, near_ref, near_s, near_r, second, count_second, lambda i: (first, i))
    share(*group_near)
    summed = near_ref[0]
    for i in range(1, count_second):
        summed = summed + near_ref[i]
    far_ref[first] = summed
    group_far = (far_ref, far_ref, far_s, far_r, first, count_first, lambda i: (i, second))
    share(*group_far)
    summed = far_ref[0]
    for i in range(1, count_first):
        summed = summed + far_ref[i]
    summed = summed * (1.0 / total_rows)
    inner = jnp.concatenate([summed[:, 0:64], summed[:, 64:128]], 0)
    proj = inner[0:KB, KB:]
    proj_ref[...] = proj
    mixed = inner[KB:, 0:KB]
    twice = 2.0 * proj - jnp.dot(inner[0:KB, 0:KB], proj, precision=highest, preferred_element_type=jnp.float32)
    gram = inner[KB:, KB:] - jnp.dot(mixed, twice, precision=highest, preferred_element_type=jnp.float32)

    row_at = lax.broadcasted_iota(jnp.int32, (BLK, LANES), 0)
    lane_at = lax.broadcasted_iota(jnp.int32, (BLK, LANES), 1)
    unit = jnp.where(row_at == lane_at, 1.0, 0.0)
    left = jnp.concatenate(
        [gram, -mixed, unit[:, 0:BLK], jnp.zeros((BLK, LANES - 2 * BLK - KB), jnp.float32)], 1
    )
    solved = jnp.zeros((BLK, LANES), jnp.float32)
    for j in range(BLK):
        pivot = jnp.sqrt(left[j : j + 1, j : j + 1])
        row = left[j : j + 1, :] / pivot
        column = left[:, j : j + 1] / pivot
        solved = jnp.where(row_at == j, row, solved)
        left = left - jnp.where(row_at > j, column * row, 0.0)
    upper_ref[...] = jnp.where(lane_at >= row_at, solved, 0.0)[:, 0:BLK]
    ortho_ref[...] = jnp.dot(
        solved[:, BLK : 2 * BLK + KB], stack_ref[...], precision=highest, preferred_element_type=jnp.float32
    )
    exchange_drain(*group)
    drain_share(*group_near)
    drain_share(*group_far)


def share(held, _, sends, recvs, me, count, place):
    def start(d, carry):
        to = lax.rem(me + d, count)
        remote(held.at[me], held.at[me], sends.at[to], recvs.at[me], place(to)).start()
        return carry

    def wait(d, carry):
        source = lax.rem(me + count - d, count)
        remote(held.at[source], held.at[source], sends.at[source], recvs.at[source], place(source)).wait_recv()
        return carry

    lax.fori_loop(1, count, start, 0)
    lax.fori_loop(1, count, wait, 0)


def drain_share(held, _, sends, recvs, me, count, place):
    def drain(d, carry):
        to = lax.rem(me + d, count)
        remote(held.at[me], held.at[me], sends.at[to], recvs.at[me], place(to)).wait_send()
        return carry

    lax.fori_loop(1, count, drain, 0)


def vmem():
    return pl.BlockSpec(memory_space=pltpu.VMEM)


def smem():
    return pl.BlockSpec(memory_space=pltpu.SMEM)


def params(collective=None):
    if collective is None:
        return pltpu.CompilerParams(vmem_limit_bytes=VMEM_BYTES)
    return pltpu.CompilerParams(
        vmem_limit_bytes=VMEM_BYTES, collective_id=collective, has_side_effects=True
    )


def cost(micros):
    return pl.CostEstimate(flops=0, bytes_accessed=int(micros * 3.6e6), transcendentals=0)


def semaphores(count, pairs):
    return [pltpu.SemaphoreType.DMA((count,))] * (2 * pairs)


def body(basis, velocity, temper, flags, order):
    count_first = lax.axis_size("bxy")
    count_second = lax.axis_size("bz")
    devices = count_first * count_second
    panel_rows = basis.shape[1]
    piece = panel_rows // count_first
    slab_rows = piece * devices
    total_rows = panel_rows * devices
    tall, third = temper.shape[1:]
    ways = count_second // CORES
    vecs = BLK // ways
    parts = count_first // vecs
    high = tall // CORES // parts
    wide = -(-(tall // CORES + 4) // 8) * 8
    piece_wide = -(-(high + 4) // 8) * 8
    padded = -(-piece // LANES) * LANES
    panels = devices // CORES
    me_first = lax.axis_index("bxy")
    core = lax.rem(lax.axis_index("bz"), CORES)

    height = lax.broadcasted_iota(jnp.int32, temper.shape, 1)
    solid = (flags == 1) | (height == 0) | (height == tall - 1)
    base = jnp.concatenate([velocity, temper[None], solid.astype(jnp.float32)[None]], 0)
    base = base.transpose(1, 0, 2, 3)
    ring = jnp.concatenate([base[:, :, tall - 2 :], base, base[:, :, : wide]], 2)
    ring = lax.dynamic_slice_in_dim(ring, core * (tall // CORES), wide, 2)
    ring = lax.all_gather(ring, "bxy", axis=0, tiled=True)
    part = me_first // vecs
    if parts > 1:
        ring = jnp.concatenate([ring, ring[:, :, :8]], 2)
        ring = lax.dynamic_slice_in_dim(ring, part * high, piece_wide, 2)

    outgoing = basis[KB - BLK :].reshape(ways, vecs, count_first, piece).transpose(2, 0, 1, 3)
    outgoing = jnp.pad(outgoing, ((0, 0), (0, 0), (0, 0), (0, padded - piece)))
    outgoing = outgoing.reshape(panels, vecs, padded)
    arrived = pl.pallas_call(
        functools.partial(panels_kernel, ways),
        out_shape=jax.ShapeDtypeStruct((panels, vecs, padded), jnp.float32),
        in_specs=[vmem()],
        out_specs=vmem(),
        scratch_shapes=semaphores(panels, 1),
        compiler_params=params(0),
        cost_estimate=cost(12),
    )(outgoing)
    part_shape = jax.ShapeDtypeStruct((vecs, 5, wide, third), jnp.float32)
    mine, other = pl.pallas_call(
        functools.partial(spread_kernel, piece, tall),
        out_shape=(part_shape, part_shape),
        in_specs=[smem(), vmem()],
        out_specs=(vmem(), vmem()),
        scratch_shapes=[
            pltpu.VMEM((padded, LANES), jnp.float32),
            pltpu.VMEM((slab_rows, LANES), jnp.float32),
        ],
        compiler_params=params(),
        cost_estimate=cost(28),
    )(order, arrived)
    if parts > 1:
        mine, other = [
            jnp.concatenate([array[:, :, s * high : s * high + piece_wide] for s in range(parts)], 0)
            for array in (mine, other)
        ]
    block = (count_first, 5, piece_wide, third)
    fields = pl.pallas_call(
        gather_kernel,
        out_shape=jax.ShapeDtypeStruct(block, jnp.float32),
        in_specs=[vmem(), vmem()],
        out_specs=vmem(),
        scratch_shapes=[pltpu.VMEM(block, jnp.float32)] * 2 + semaphores(count_first, 2),
        compiler_params=params(1),
        cost_estimate=cost(12),
    )(mine, other)

    state = pltpu.VMEM((26, count_first, piece_wide, third), jnp.float32)
    evolved = pl.pallas_call(
        functools.partial(lattice_kernel, count_first, high),
        out_shape=jax.ShapeDtypeStruct((count_first, 5, high, third), jnp.float32),
        in_specs=[vmem(), vmem()],
        out_specs=vmem(),
        scratch_shapes=[state, state],
        compiler_params=params(),
    )(fields, ring)

    half_shape = jax.ShapeDtypeStruct((count_first, 5, high, third), jnp.float32)
    back, back_other = pl.pallas_call(
        scatter_kernel,
        out_shape=(half_shape, half_shape),
        in_specs=[vmem()],
        out_specs=(vmem(), vmem()),
        scratch_shapes=semaphores(count_first, 2),
        compiler_params=params(2),
        cost_estimate=cost(12),
    )(evolved)
    if parts > 1:
        back, back_other = [
            array.reshape(parts, vecs, 5, high, third)
            .transpose(1, 2, 0, 3, 4)
            .reshape(vecs, 5, parts * high, third)
            for array in (back, back_other)
        ]
    leaving = pl.pallas_call(
        functools.partial(collect_kernel, piece, tall),
        out_shape=jax.ShapeDtypeStruct((panels, vecs, padded), jnp.float32),
        in_specs=[smem(), vmem(), vmem()],
        out_specs=vmem(),
        scratch_shapes=[
            pltpu.VMEM((padded, LANES), jnp.float32),
            pltpu.VMEM((slab_rows, LANES), jnp.float32),
        ],
        compiler_params=params(),
        cost_estimate=cost(28),
    )(order, back, back_other)
    return pl.pallas_call(
        functools.partial(project_kernel, ways, piece, total_rows),
        out_shape=(
            jax.ShapeDtypeStruct((BLK, panel_rows), jnp.float32),
            jax.ShapeDtypeStruct((KB, BLK), jnp.float32),
            jax.ShapeDtypeStruct((BLK, BLK), jnp.float32),
        ),
        in_specs=[vmem(), vmem()],
        out_specs=(vmem(), vmem(), vmem()),
        scratch_shapes=[
            pltpu.VMEM((panels, vecs, padded), jnp.float32),
            pltpu.VMEM((KB + BLK, panel_rows), jnp.float32),
            pltpu.VMEM((count_second, 32, LANES), jnp.float32),
            pltpu.VMEM((count_first, 32, LANES), jnp.float32),
        ]
        + semaphores(panels, 1)
        + semaphores(count_second, 1)
        + semaphores(count_first, 1),
        compiler_params=params(3),
        cost_estimate=cost(20),
    )(leaving, basis)


def solution(mesh):
    in_specs = (
        P(None, ("bxy", "bz")),
        P(None, "bxy", None, None),
        P("bxy", None, None),
        P("bxy", None, None),
        P("bxy", None),
    )
    out_specs = (P(None, ("bxy", "bz")), P(), P())
    return jax.shard_map(body, mesh=mesh, in_specs=in_specs, out_specs=out_specs, check_vma=False)
```

```python
import functools

import jax
import jax.numpy as jnp
from jax import lax
from jax.experimental import pallas as pl
from jax.experimental.pallas import tpu as pltpu
from jax.sharding import PartitionSpec as P

BLK = 16
KB = 48
CORES = 2
LANES = 128
VMEM_BYTES = 56 * 1024 * 1024


FLOW_DIRS = (
    (0, 0, 0),
    (1, 0, 0),
    (-1, 0, 0),
    (0, 1, 0),
    (0, -1, 0),
    (0, 0, 1),
    (0, 0, -1),
    (1, 1, 0),
    (-1, -1, 0),
    (1, -1, 0),
    (-1, 1, 0),
    (1, 0, 1),
    (-1, 0, -1),
    (1, 0, -1),
    (-1, 0, 1),
    (0, 1, 1),
    (0, -1, -1),
    (0, 1, -1),
    (0, -1, 1),
)
ALL_DIRS = FLOW_DIRS + FLOW_DIRS[:7]
FLOW_WEIGHTS = (1.0 / 3.0,) + (1.0 / 18.0,) * 6 + (1.0 / 36.0,) * 12
HEAT_WEIGHTS = (0.25,) + (0.125,) * 6
OPPOSITE = (0,) + tuple((number + 1 if number % 2 == 1 else number - 1 for number in range(1, 19)))
OMEGA_FLOW = 1.6
OMEGA_HEAT = 1.4
BUOYANCY = 0.2


def along(direction, comps):
    total = None
    for weight, array in zip(direction, comps):
        if weight == 1:
            total = array if total is None else total + array
        elif weight == -1:
            total = -array if total is None else total - array
    return total


def moments(flow, heat):
    density = flow[0]
    for number in range(1, 19):
        density = density + flow[number]
    momentum = []
    for comp in range(3):
        momentum.append(along([FLOW_DIRS[number][comp] for number in range(19)], flow))
    warmth = heat[0]
    for number in range(1, 7):
        warmth = warmth + heat[number]
    return (density, momentum, warmth)


def equilibria(density, momentum, warmth, velocity, temper):
    carried = [momentum[comp] - velocity[comp] * density for comp in range(3)]
    speed_sq = velocity[0] * velocity[0] + velocity[1] * velocity[1] + velocity[2] * velocity[2]
    carried_u = velocity[0] * carried[0] + velocity[1] * carried[1] + velocity[2] * carried[2]
    rest = density * (1.0 - 1.5 * speed_sq) - 3.0 * carried_u
    flow_eq = [FLOW_WEIGHTS[0] * rest] + [None] * 18
    heat_eq = [HEAT_WEIGHTS[0] * warmth] + [None] * 6
    for number in range(1, 19, 2):
        drift = along(FLOW_DIRS[number], velocity)
        push = along(FLOW_DIRS[number], carried)
        even = rest + drift * (4.5 * drift * density + 9.0 * push)
        odd = 3.0 * (drift * density + push)
        flow_eq[number] = FLOW_WEIGHTS[number] * (even + odd)
        flow_eq[number + 1] = FLOW_WEIGHTS[number] * (even - odd)
        if number < 7:
            tilt = 4.0 * (warmth * drift + temper * push)
            heat_eq[number] = HEAT_WEIGHTS[number] * (warmth + tilt)
            heat_eq[number + 1] = HEAT_WEIGHTS[number] * (warmth - tilt)
    return (flow_eq, heat_eq)


def lattice_kernel(count, high, fields_ref, base_ref, out_ref, first_ref, second_ref):
    wide = fields_ref.shape[2]

    me = lax.axis_index("bxy")

    def base_at(place):
        x = lax.rem(me + count - place, count)
        return (
            [base_ref[x, 0], base_ref[x, 1], base_ref[x, 2]],
            base_ref[x, 3],
            base_ref[x, 4] > 0.5,
        )

    def force(number, warmth):
        return 3.0 * FLOW_WEIGHTS[number] * FLOW_DIRS[number][1] * BUOYANCY * warmth

    def streamed(ref, x):
        found = []
        for number in range(26):
            first, second, third = ALL_DIRS[number]
            value = ref[number, lax.rem(x + count - first, count)]
            if second:
                value = pltpu.roll(value, second % wide, 0)
            if third:
                value = pltpu.roll(value, third % LANES, 1)
            found.append(value)
        return (found[:19], found[19:])

    def begin(x, carry):
        velocity, temper, solid = base_at(x)
        warmth = fields_ref[x, 4]
        flow, heat = equilibria(
            fields_ref[x, 0],
            [fields_ref[x, 1], fields_ref[x, 2], fields_ref[x, 3]],
            warmth,
            velocity,
            temper,
        )
        for number in range(19):
            fresh = flow[number]
            if FLOW_DIRS[number][1]:
                fresh = fresh + force(number, warmth)
            first_ref[number, x] = jnp.where(solid, flow[OPPOSITE[number]], fresh)
        for number in range(7):
            first_ref[19 + number, x] = jnp.where(solid, heat[OPPOSITE[number]], heat[number])
        return carry

    def again(x, carry):
        velocity, temper, solid = base_at(x)
        flow, heat = streamed(first_ref, x)
        density, momentum, warmth = moments(flow, heat)
        flow_eq, heat_eq = equilibria(density, momentum, warmth, velocity, temper)
        for number in range(19):
            fresh = (1.0 - OMEGA_FLOW) * flow[number] + OMEGA_FLOW * flow_eq[number]
            if FLOW_DIRS[number][1]:
                fresh = fresh + force(number, warmth)
            second_ref[number, x] = jnp.where(solid, flow[OPPOSITE[number]], fresh)
        for number in range(7):
            fresh = (1.0 - OMEGA_HEAT) * heat[number] + OMEGA_HEAT * heat_eq[number]
            second_ref[19 + number, x] = jnp.where(solid, heat[OPPOSITE[number]], fresh)
        return carry

    def finish(x, carry):
        flow, heat = streamed(second_ref, x)
        density, momentum, warmth = moments(flow, heat)
        for number, value in enumerate([density] + momentum + [warmth]):
            out_ref[x, number] = value[2 : 2 + high]
        return carry

    lax.fori_loop(0, count, begin, 0)
    lax.fori_loop(0, count, again, 0)
    lax.fori_loop(0, count, finish, 0)


def spread_kernel(piece, tall, order_ref, arrived_ref, mine_ref, other_ref, rows_ref, spread_ref):
    core = lax.rem(lax.axis_index("bz"), CORES)
    panels, vecs, padded = arrived_ref.shape
    step = next(size for size in (48, 40, 32, 16, 8) if piece % size == 0)
    wide = mine_ref.shape[2]
    half = tall // CORES
    total = spread_ref.shape[0]

    def clear(i, carry):
        spread_ref[pl.ds(pl.multiple_of(i * 256, 256), 256), :] = jnp.zeros((256, LANES), jnp.float32)
        return carry

    lax.fori_loop(0, total // 256, clear, 0)

    def panel(i, carry):
        for start in range(0, padded, LANES):
            rows_ref[start : start + LANES, 0:vecs] = arrived_ref[i, :, start : start + LANES].T
        base = (CORES * i + core) * piece

        def rows(j, carry):
            at = pl.multiple_of(j * step, 8)
            held = [rows_ref[pl.ds(at + t, 1), :] for t in range(step)]
            for t in range(step):
                spread_ref[pl.ds(order_ref[0, base + at + t], 1), :] = held[t]
            return carry

        return lax.fori_loop(0, piece // step, rows, carry)

    lax.fori_loop(0, panels, panel, 0)

    for out_ref, which in ((mine_ref, core), (other_ref, 1 - core)):

        def moment(m, carry):
            for r in range(wide):
                level = lax.rem(half * which + tall - 2 + r, tall)
                start = pl.multiple_of((m * tall + level) * LANES, LANES)
                block = spread_ref[pl.ds(start, LANES), :].T
                for v in range(vecs):
                    out_ref[v, m, r : r + 1, :] = block[v : v + 1, :]
            return carry

        lax.fori_loop(0, 5, moment, 0)


def exchange_start(send, out_ref, sends, recvs, me, count, place):
    def start(d, carry):
        to = lax.rem(me + d, count)
        remote(send.at[to], out_ref.at[me], sends.at[to], recvs.at[me], place(to)).start()
        return carry

    lax.fori_loop(1, count, start, 0)


def exchange_wait(send, out_ref, sends, recvs, me, count, place, then=None):
    def wait(d, carry):
        source = lax.rem(me + count - d, count)
        remote(send.at[source], out_ref.at[source], sends.at[source], recvs.at[source], place(source)).wait_recv()
        if then is not None:
            then(source)
        return carry

    lax.fori_loop(1, count, wait, 0)


def exchange_drain(send, out_ref, sends, recvs, me, count, place):
    def drain(d, carry):
        to = lax.rem(me + d, count)
        remote(send.at[to], out_ref.at[me], sends.at[to], recvs.at[me], place(to)).wait_send()
        return carry

    lax.fori_loop(1, count, drain, 0)


def remote(source, target, send, recv, place):
    return pltpu.make_async_remote_copy(
        src_ref=source,
        dst_ref=target,
        send_sem=send,
        recv_sem=recv,
        device_id=place,
        device_id_type=pl.DeviceIdType.MESH,
    )


def greet(me, count, place):
    barrier = pltpu.get_barrier_semaphore()

    def hello(d, carry):
        pl.semaphore_signal(
            barrier, inc=1, device_id=place(lax.rem(me + d, count)), device_id_type=pl.DeviceIdType.MESH
        )
        return carry

    lax.fori_loop(1, count, hello, 0)


def position():
    first, second = lax.axis_index("bxy"), lax.axis_index("bz")
    return (first, second, lax.rem(second, CORES), second // CORES)


def panels_kernel(ways, outgoing_ref, arrived_ref, sends, recvs):
    first, _, core, way = position()
    count = outgoing_ref.shape[0]
    me = first * ways + way

    def place(i):
        return (i // ways, lax.rem(i, ways) * CORES + core)

    greet(me, count, place)
    pl.semaphore_wait(pltpu.get_barrier_semaphore(), count - 1)
    group = (outgoing_ref, arrived_ref, sends, recvs, me, count, place)
    exchange_start(*group)
    arrived_ref[me] = outgoing_ref[me]
    exchange_wait(*group)
    exchange_drain(*group)


def gather_kernel(mine_ref, other_ref, out_ref, got_ref, mix_ref, swap_s, swap_r, sends, recvs):
    me, second, core, _ = position()
    count = mine_ref.shape[0]
    sibling = (me, second + 1 - 2 * core)

    def place(i):
        return (i, second)

    greet(me, count, place)
    barrier = pltpu.get_barrier_semaphore()
    pl.semaphore_signal(barrier, inc=1, device_id=sibling, device_id_type=pl.DeviceIdType.MESH)
    pl.semaphore_wait(barrier, count)

    def swap(i):
        return remote(other_ref.at[i], got_ref.at[i], swap_s.at[i], swap_r.at[i], sibling)

    def begin(d, carry):
        swap(lax.rem(me + d, count)).start()
        return carry

    lax.fori_loop(1, count + 1, begin, 0)

    def send(d, carry):
        to = lax.rem(me + d, count)
        swap(to).wait_recv()
        mix_ref[to] = mine_ref[to] + got_ref[to]
        remote(mix_ref.at[to], out_ref.at[me], sends.at[to], recvs.at[me], place(to)).start()
        return carry

    lax.fori_loop(1, count, send, 0)
    swap(me).wait_recv()
    out_ref[me] = mine_ref[me] + got_ref[me]
    group = (mix_ref, out_ref, sends, recvs, me, count, place)
    exchange_wait(*group)
    exchange_drain(*group)

    def end(i, carry):
        swap(i).wait_send()
        return carry

    lax.fori_loop(0, count, end, 0)


def scatter_kernel(evolved_ref, mine_ref, other_ref, swap_s, swap_r, sends, recvs):
    me, second, core, _ = position()
    count = evolved_ref.shape[0]
    sibling = (me, second + 1 - 2 * core)

    def place(i):
        return (i, second)

    greet(me, count, place)
    barrier = pltpu.get_barrier_semaphore()
    pl.semaphore_signal(barrier, inc=1, device_id=sibling, device_id_type=pl.DeviceIdType.MESH)
    pl.semaphore_wait(barrier, count)

    def swap(i):
        return remote(mine_ref.at[i], other_ref.at[i], swap_s.at[i], swap_r.at[i], sibling)

    group = (evolved_ref, mine_ref, sends, recvs, me, count, place)
    exchange_start(*group)
    mine_ref[me] = evolved_ref[me]
    swap(me).start()
    exchange_wait(*group, then=lambda source: swap(source).start())
    exchange_drain(*group)

    def end(i, carry):
        swap(i).wait()
        return carry

    lax.fori_loop(0, count, end, 0)


def project_kernel(
    ways, piece, tall, total_rows, order_ref, mine_ref, other_ref, basis_ref, ortho_ref, proj_ref, upper_ref,
    rows_ref, table_ref, leaving_ref, landed_ref, stack_ref, near_ref, far_ref, sends, recvs, near_s, near_r, far_s, far_r,
):
    first, second, core, way = position()
    count = leaving_ref.shape[0]
    count_second, count_first = near_ref.shape[0], far_ref.shape[0]
    vecs = BLK // ways
    me = first * ways + way

    def place(i):
        return (i // ways, lax.rem(i, ways) * CORES + core)

    greet(me, count, place)
    barrier = pltpu.get_barrier_semaphore()
    for k in range(ways):
        pl.semaphore_signal(
            barrier, inc=1, device_id=(first, k * CORES + 1 - core), device_id_type=pl.DeviceIdType.MESH
        )
    pl.semaphore_wait(barrier, count - 1 + ways)
    group = (leaving_ref, landed_ref, sends, recvs, me, count, place)
    padded = leaving_ref.shape[2]
    half = tall // CORES
    step = next(size for size in (48, 40, 32, 16, 8) if piece % size == 0)

    for in_ref, which in ((mine_ref, core), (other_ref, 1 - core)):

        def moment(m, carry):
            for r in range(half):
                start = pl.multiple_of((m * tall + half * which + r) * LANES, LANES)
                block = jnp.concatenate([in_ref[v, m, r : r + 1, :] for v in range(vecs)], 0)
                table_ref[pl.ds(start, LANES), 0:vecs] = block.T
            return carry

        lax.fori_loop(0, 5, moment, 0)

    if padded > piece:
        rows_ref[piece:padded, :] = jnp.zeros((padded - piece, LANES), jnp.float32)

    def collect(i):
        base = (CORES * i + core) * piece

        def rows(j, carry):
            at = pl.multiple_of(j * step, 8)
            held = [table_ref[pl.ds(order_ref[0, base + at + t], 1), :] for t in range(step)]
            for t in range(step):
                rows_ref[pl.ds(at + t, 1), :] = held[t]
            return carry

        lax.fori_loop(0, piece // step, rows, 0)
        for start in range(0, padded, LANES):
            block = rows_ref[start : start + LANES, :].T
            leaving_ref[i, :, start : start + LANES] = block[0:vecs, :]

    def panel(d, carry):
        to = lax.rem(me + d, count)
        collect(to)
        remote(leaving_ref.at[to], landed_ref.at[me], sends.at[to], recvs.at[me], place(to)).start()
        return carry

    lax.fori_loop(1, count, panel, 0)
    collect(me)
    landed_ref[me] = leaving_ref[me]
    stack_ref[0:KB] = basis_ref[...]
    exchange_wait(*group)
    for p in range(count_first):
        for k in range(ways):
            stack_ref[KB + k * vecs : KB + (k + 1) * vecs, p * piece : (p + 1) * piece] = landed_ref[
                p * ways + k, :, 0:piece
            ]
    highest = lax.Precision.HIGHEST
    across = (((1,), (1,)), ((), ()))
    stack = stack_ref[...]
    inner = lax.dot_general(stack, stack, across, precision=highest, preferred_element_type=jnp.float32)

    near_ref[second] = jnp.concatenate([inner[0:32], inner[32:64]], 1)
    group_near = (near_ref, near_ref, near_s, near_r, second, count_second, lambda i: (first, i))
    share(*group_near)
    summed = near_ref[0]
    for i in range(1, count_second):
        summed = summed + near_ref[i]
    far_ref[first] = summed
    group_far = (far_ref, far_ref, far_s, far_r, first, count_first, lambda i: (i, second))
    share(*group_far)
    summed = far_ref[0]
    for i in range(1, count_first):
        summed = summed + far_ref[i]
    summed = summed * (1.0 / total_rows)
    inner = jnp.concatenate([summed[:, 0:64], summed[:, 64:128]], 0)
    proj = inner[0:KB, KB:]
    proj_ref[...] = proj
    mixed = inner[KB:, 0:KB]
    twice = 2.0 * proj - jnp.dot(inner[0:KB, 0:KB], proj, precision=highest, preferred_element_type=jnp.float32)
    gram = inner[KB:, KB:] - jnp.dot(mixed, twice, precision=highest, preferred_element_type=jnp.float32)

    row_at = lax.broadcasted_iota(jnp.int32, (BLK, LANES), 0)
    lane_at = lax.broadcasted_iota(jnp.int32, (BLK, LANES), 1)
    unit = jnp.where(row_at == lane_at, 1.0, 0.0)
    left = jnp.concatenate(
        [gram, -mixed, unit[:, 0:BLK], jnp.zeros((BLK, LANES - 2 * BLK - KB), jnp.float32)], 1
    )
    solved = jnp.zeros((BLK, LANES), jnp.float32)
    for j in range(BLK):
        pivot = jnp.sqrt(left[j : j + 1, j : j + 1])
        row = left[j : j + 1, :] / pivot
        column = left[:, j : j + 1] / pivot
        solved = jnp.where(row_at == j, row, solved)
        left = left - jnp.where(row_at > j, column * row, 0.0)
    upper_ref[...] = jnp.where(lane_at >= row_at, solved, 0.0)[:, 0:BLK]
    ortho_ref[...] = jnp.dot(
        solved[:, BLK : 2 * BLK + KB], stack_ref[...], precision=highest, preferred_element_type=jnp.float32
    )
    exchange_drain(*group)
    drain_share(*group_near)
    drain_share(*group_far)


def share(held, _, sends, recvs, me, count, place):
    def start(d, carry):
        to = lax.rem(me + d, count)
        remote(held.at[me], held.at[me], sends.at[to], recvs.at[me], place(to)).start()
        return carry

    def wait(d, carry):
        source = lax.rem(me + count - d, count)
        remote(held.at[source], held.at[source], sends.at[source], recvs.at[source], place(source)).wait_recv()
        return carry

    lax.fori_loop(1, count, start, 0)
    lax.fori_loop(1, count, wait, 0)


def drain_share(held, _, sends, recvs, me, count, place):
    def drain(d, carry):
        to = lax.rem(me + d, count)
        remote(held.at[me], held.at[me], sends.at[to], recvs.at[me], place(to)).wait_send()
        return carry

    lax.fori_loop(1, count, drain, 0)


def vmem():
    return pl.BlockSpec(memory_space=pltpu.VMEM)


def smem():
    return pl.BlockSpec(memory_space=pltpu.SMEM)


def params(collective=None):
    if collective is None:
        return pltpu.CompilerParams(vmem_limit_bytes=VMEM_BYTES)
    return pltpu.CompilerParams(
        vmem_limit_bytes=VMEM_BYTES, collective_id=collective, has_side_effects=True
    )


def cost(micros):
    return pl.CostEstimate(flops=0, bytes_accessed=int(micros * 3.6e6), transcendentals=0)


def semaphores(count, pairs):
    return [pltpu.SemaphoreType.DMA((count,))] * (2 * pairs)


def body(basis, velocity, temper, flags, order):
    count_first = lax.axis_size("bxy")
    count_second = lax.axis_size("bz")
    devices = count_first * count_second
    panel_rows = basis.shape[1]
    piece = panel_rows // count_first
    slab_rows = piece * devices
    total_rows = panel_rows * devices
    tall, third = temper.shape[1:]
    ways = count_second // CORES
    vecs = BLK // ways
    parts = count_first // vecs
    high = tall // CORES // parts
    wide = -(-(tall // CORES + 4) // 8) * 8
    piece_wide = -(-(high + 4) // 8) * 8
    padded = -(-piece // LANES) * LANES
    panels = devices // CORES
    me_first = lax.axis_index("bxy")
    core = lax.rem(lax.axis_index("bz"), CORES)

    height = lax.broadcasted_iota(jnp.int32, temper.shape, 1)
    solid = (flags == 1) | (height == 0) | (height == tall - 1)
    base = jnp.concatenate([velocity, temper[None], solid.astype(jnp.float32)[None]], 0)
    base = base.transpose(1, 0, 2, 3)
    ring = jnp.concatenate([base[:, :, tall - 2 :], base, base[:, :, : wide]], 2)
    ring = lax.dynamic_slice_in_dim(ring, core * (tall // CORES), wide, 2)
    rings = [ring] + [
        lax.ppermute(ring, "bxy", [(i, (i + d) % count_first) for i in range(count_first)])
        for d in range(1, count_first)
    ]

    outgoing = basis[KB - BLK :].reshape(ways, vecs, count_first, piece).transpose(2, 0, 1, 3)
    outgoing = jnp.pad(outgoing, ((0, 0), (0, 0), (0, 0), (0, padded - piece)))
    outgoing = outgoing.reshape(panels, vecs, padded)
    arrived = pl.pallas_call(
        functools.partial(panels_kernel, ways),
        out_shape=jax.ShapeDtypeStruct((panels, vecs, padded), jnp.float32),
        in_specs=[vmem()],
        out_specs=vmem(),
        scratch_shapes=semaphores(panels, 1),
        compiler_params=params(0),
        cost_estimate=cost(12),
    )(outgoing)
    part_shape = jax.ShapeDtypeStruct((vecs, 5, wide, third), jnp.float32)
    mine, other = pl.pallas_call(
        functools.partial(spread_kernel, piece, tall),
        out_shape=(part_shape, part_shape),
        in_specs=[smem(), vmem()],
        out_specs=(vmem(), vmem()),
        scratch_shapes=[
            pltpu.VMEM((padded, LANES), jnp.float32),
            pltpu.VMEM((slab_rows, LANES), jnp.float32),
        ],
        compiler_params=params(),
        cost_estimate=cost(28),
    )(order, arrived)
    held = lax.optimization_barrier((mine, other, *rings))
    mine, other = held[:2]
    ring = jnp.concatenate(held[2:], 0)
    part = me_first // vecs
    if parts > 1:
        ring = lax.dynamic_slice_in_dim(ring, part * high, piece_wide, 2)
        mine, other = [
            jnp.concatenate([array[:, :, s * high : s * high + piece_wide] for s in range(parts)], 0)
            for array in (mine, other)
        ]
    block = (count_first, 5, piece_wide, third)
    fields = pl.pallas_call(
        gather_kernel,
        out_shape=jax.ShapeDtypeStruct(block, jnp.float32),
        in_specs=[vmem(), vmem()],
        out_specs=vmem(),
        scratch_shapes=[pltpu.VMEM(block, jnp.float32)] * 2 + semaphores(count_first, 2),
        compiler_params=params(1),
        cost_estimate=cost(12),
    )(mine, other)

    state = pltpu.VMEM((26, count_first, piece_wide, third), jnp.float32)
    evolved = pl.pallas_call(
        functools.partial(lattice_kernel, count_first, high),
        out_shape=jax.ShapeDtypeStruct((count_first, 5, high, third), jnp.float32),
        in_specs=[vmem(), vmem()],
        out_specs=vmem(),
        scratch_shapes=[state, state],
        compiler_params=params(),
    )(fields, ring)

    half_shape = jax.ShapeDtypeStruct((count_first, 5, high, third), jnp.float32)
    back, back_other = pl.pallas_call(
        scatter_kernel,
        out_shape=(half_shape, half_shape),
        in_specs=[vmem()],
        out_specs=(vmem(), vmem()),
        scratch_shapes=semaphores(count_first, 2),
        compiler_params=params(2),
        cost_estimate=cost(12),
    )(evolved)
    if parts > 1:
        back, back_other = [
            array.reshape(parts, vecs, 5, high, third)
            .transpose(1, 2, 0, 3, 4)
            .reshape(vecs, 5, parts * high, third)
            for array in (back, back_other)
        ]
    return pl.pallas_call(
        functools.partial(project_kernel, ways, piece, tall, total_rows),
        out_shape=(
            jax.ShapeDtypeStruct((BLK, panel_rows), jnp.float32),
            jax.ShapeDtypeStruct((KB, BLK), jnp.float32),
            jax.ShapeDtypeStruct((BLK, BLK), jnp.float32),
        ),
        in_specs=[smem(), vmem(), vmem(), vmem()],
        out_specs=(vmem(), vmem(), vmem()),
        scratch_shapes=[
            pltpu.VMEM((padded, LANES), jnp.float32),
            pltpu.VMEM((slab_rows, LANES), jnp.float32),
            pltpu.VMEM((panels, vecs, padded), jnp.float32),
            pltpu.VMEM((panels, vecs, padded), jnp.float32),
            pltpu.VMEM((KB + BLK, panel_rows), jnp.float32),
            pltpu.VMEM((count_second, 32, LANES), jnp.float32),
            pltpu.VMEM((count_first, 32, LANES), jnp.float32),
        ]
        + semaphores(panels, 1)
        + semaphores(count_second, 1)
        + semaphores(count_first, 1),
        compiler_params=params(3),
        cost_estimate=cost(50),
    )(order, back, back_other, basis)


def solution(mesh):
    in_specs = (
        P(None, ("bxy", "bz")),
        P(None, "bxy", None, None),
        P("bxy", None, None),
        P("bxy", None, None),
        P("bxy", None),
    )
    out_specs = (P(None, ("bxy", "bz")), P(), P())
    return jax.shard_map(body, mesh=mesh, in_specs=in_specs, out_specs=out_specs, check_vma=False)
```

```python
import functools

import jax
import jax.numpy as jnp
from jax import lax
from jax.experimental import pallas as pl
from jax.experimental.pallas import tpu as pltpu
from jax.sharding import PartitionSpec as P

BLK = 16
KB = 48
CORES = 2
LANES = 128
VMEM_BYTES = 56 * 1024 * 1024


FLOW_DIRS = (
    (0, 0, 0),
    (1, 0, 0),
    (-1, 0, 0),
    (0, 1, 0),
    (0, -1, 0),
    (0, 0, 1),
    (0, 0, -1),
    (1, 1, 0),
    (-1, -1, 0),
    (1, -1, 0),
    (-1, 1, 0),
    (1, 0, 1),
    (-1, 0, -1),
    (1, 0, -1),
    (-1, 0, 1),
    (0, 1, 1),
    (0, -1, -1),
    (0, 1, -1),
    (0, -1, 1),
)
ALL_DIRS = FLOW_DIRS + FLOW_DIRS[:7]
FLOW_WEIGHTS = (1.0 / 3.0,) + (1.0 / 18.0,) * 6 + (1.0 / 36.0,) * 12
HEAT_WEIGHTS = (0.25,) + (0.125,) * 6
OPPOSITE = (0,) + tuple((number + 1 if number % 2 == 1 else number - 1 for number in range(1, 19)))
OMEGA_FLOW = 1.6
OMEGA_HEAT = 1.4
BUOYANCY = 0.2


def along(direction, comps):
    total = None
    for weight, array in zip(direction, comps):
        if weight == 1:
            total = array if total is None else total + array
        elif weight == -1:
            total = -array if total is None else total - array
    return total


def moments(flow, heat):
    density = flow[0]
    for number in range(1, 19):
        density = density + flow[number]
    momentum = []
    for comp in range(3):
        momentum.append(along([FLOW_DIRS[number][comp] for number in range(19)], flow))
    warmth = heat[0]
    for number in range(1, 7):
        warmth = warmth + heat[number]
    return (density, momentum, warmth)


def equilibria(density, momentum, warmth, velocity, temper):
    carried = [momentum[comp] - velocity[comp] * density for comp in range(3)]
    speed_sq = velocity[0] * velocity[0] + velocity[1] * velocity[1] + velocity[2] * velocity[2]
    carried_u = velocity[0] * carried[0] + velocity[1] * carried[1] + velocity[2] * carried[2]
    rest = density * (1.0 - 1.5 * speed_sq) - 3.0 * carried_u
    flow_eq = [FLOW_WEIGHTS[0] * rest] + [None] * 18
    heat_eq = [HEAT_WEIGHTS[0] * warmth] + [None] * 6
    for number in range(1, 19, 2):
        drift = along(FLOW_DIRS[number], velocity)
        push = along(FLOW_DIRS[number], carried)
        even = rest + drift * (4.5 * drift * density + 9.0 * push)
        odd = 3.0 * (drift * density + push)
        flow_eq[number] = FLOW_WEIGHTS[number] * (even + odd)
        flow_eq[number + 1] = FLOW_WEIGHTS[number] * (even - odd)
        if number < 7:
            tilt = 4.0 * (warmth * drift + temper * push)
            heat_eq[number] = HEAT_WEIGHTS[number] * (warmth + tilt)
            heat_eq[number + 1] = HEAT_WEIGHTS[number] * (warmth - tilt)
    return (flow_eq, heat_eq)


def lattice_kernel(count, high, fields_ref, base_ref, out_ref, first_ref, second_ref):
    wide = fields_ref.shape[2]

    ways = base_ref.shape[0]

    def base_at(x):
        held = [
            base_ref[0, x, m] if ways == 1 else jnp.concatenate([base_ref[k, x, m] for k in range(ways)], 0)
            for m in range(5)
        ]
        return (held[:3], held[3], held[4] > 0.5)

    def force(number, warmth):
        return 3.0 * FLOW_WEIGHTS[number] * FLOW_DIRS[number][1] * BUOYANCY * warmth

    def streamed(ref, x):
        found = []
        for number in range(26):
            first, second, third = ALL_DIRS[number]
            value = ref[number, lax.rem(x + count - first, count)]
            if second:
                value = pltpu.roll(value, second % wide, 0)
            if third:
                value = pltpu.roll(value, third % LANES, 1)
            found.append(value)
        return (found[:19], found[19:])

    def begin(x, carry):
        velocity, temper, solid = base_at(x)
        warmth = fields_ref[x, 4]
        flow, heat = equilibria(
            fields_ref[x, 0],
            [fields_ref[x, 1], fields_ref[x, 2], fields_ref[x, 3]],
            warmth,
            velocity,
            temper,
        )
        for number in range(19):
            fresh = flow[number]
            if FLOW_DIRS[number][1]:
                fresh = fresh + force(number, warmth)
            first_ref[number, x] = jnp.where(solid, flow[OPPOSITE[number]], fresh)
        for number in range(7):
            first_ref[19 + number, x] = jnp.where(solid, heat[OPPOSITE[number]], heat[number])
        return carry

    def again(x, carry):
        velocity, temper, solid = base_at(x)
        flow, heat = streamed(first_ref, x)
        density, momentum, warmth = moments(flow, heat)
        flow_eq, heat_eq = equilibria(density, momentum, warmth, velocity, temper)
        for number in range(19):
            fresh = (1.0 - OMEGA_FLOW) * flow[number] + OMEGA_FLOW * flow_eq[number]
            if FLOW_DIRS[number][1]:
                fresh = fresh + force(number, warmth)
            second_ref[number, x] = jnp.where(solid, flow[OPPOSITE[number]], fresh)
        for number in range(7):
            fresh = (1.0 - OMEGA_HEAT) * heat[number] + OMEGA_HEAT * heat_eq[number]
            second_ref[19 + number, x] = jnp.where(solid, heat[OPPOSITE[number]], fresh)
        return carry

    def finish(x, carry):
        flow, heat = streamed(second_ref, x)
        density, momentum, warmth = moments(flow, heat)
        for number, value in enumerate([density] + momentum + [warmth]):
            out_ref[x, number] = value[2 : 2 + high]
        return carry

    lax.fori_loop(0, count, begin, 0)
    lax.fori_loop(0, count, again, 0)
    lax.fori_loop(0, count, finish, 0)


def spread_kernel(piece, tall, order_ref, arrived_ref, mine_ref, other_ref, rows_ref, spread_ref):
    core = lax.rem(lax.axis_index("bz"), CORES)
    panels, vecs, padded = arrived_ref.shape
    step = next(size for size in (48, 40, 32, 16, 8) if piece % size == 0)
    wide = mine_ref.shape[2]
    half = tall // CORES
    total = spread_ref.shape[0]

    def clear(i, carry):
        spread_ref[pl.ds(pl.multiple_of(i * 256, 256), 256), :] = jnp.zeros((256, LANES), jnp.float32)
        return carry

    lax.fori_loop(0, total // 256, clear, 0)

    def panel(i, carry):
        for start in range(0, padded, LANES):
            rows_ref[start : start + LANES, 0:vecs] = arrived_ref[i, :, start : start + LANES].T
        base = (CORES * i + core) * piece

        def rows(j, carry):
            at = pl.multiple_of(j * step, 8)
            held = [rows_ref[pl.ds(at + t, 1), :] for t in range(step)]
            for t in range(step):
                spread_ref[pl.ds(order_ref[0, base + at + t], 1), :] = held[t]
            return carry

        return lax.fori_loop(0, piece // step, rows, carry)

    lax.fori_loop(0, panels, panel, 0)

    for out_ref, next_ref, which in ((mine_ref, other_ref, core), (other_ref, mine_ref, 1 - core)):

        def moment(m, carry):
            for r in range(half):
                level = lax.rem(half * which + tall - 2 + r, tall)
                start = pl.multiple_of((m * tall + level) * LANES, LANES)
                block = spread_ref[pl.ds(start, LANES), :].T
                for v in range(vecs):
                    out_ref[v, m, r : r + 1, :] = block[v : v + 1, :]
                    if half + r < wide:
                        next_ref[v, m, half + r : half + r + 1, :] = block[v : v + 1, :]
            return carry

        lax.fori_loop(0, 5, moment, 0)


def exchange_start(send, out_ref, sends, recvs, me, count, place):
    def start(d, carry):
        to = lax.rem(me + d, count)
        remote(send.at[to], out_ref.at[me], sends.at[to], recvs.at[me], place(to)).start()
        return carry

    lax.fori_loop(1, count, start, 0)


def exchange_wait(send, out_ref, sends, recvs, me, count, place, then=None):
    def wait(d, carry):
        source = lax.rem(me + count - d, count)
        remote(send.at[source], out_ref.at[source], sends.at[source], recvs.at[source], place(source)).wait_recv()
        if then is not None:
            then(source)
        return carry

    lax.fori_loop(1, count, wait, 0)


def exchange_drain(send, out_ref, sends, recvs, me, count, place):
    def drain(d, carry):
        to = lax.rem(me + d, count)
        remote(send.at[to], out_ref.at[me], sends.at[to], recvs.at[me], place(to)).wait_send()
        return carry

    lax.fori_loop(1, count, drain, 0)


def remote(source, target, send, recv, place):
    return pltpu.make_async_remote_copy(
        src_ref=source,
        dst_ref=target,
        send_sem=send,
        recv_sem=recv,
        device_id=place,
        device_id_type=pl.DeviceIdType.MESH,
    )


def greet(me, count, place):
    barrier = pltpu.get_barrier_semaphore()

    def hello(d, carry):
        pl.semaphore_signal(
            barrier, inc=1, device_id=place(lax.rem(me + d, count)), device_id_type=pl.DeviceIdType.MESH
        )
        return carry

    lax.fori_loop(1, count, hello, 0)


def position():
    first, second = lax.axis_index("bxy"), lax.axis_index("bz")
    return (first, second, lax.rem(second, CORES), second // CORES)


def panels_kernel(ways, outgoing_ref, share_ref, arrived_ref, base_ref, sends, recvs, base_s, base_r, pass_s, pass_r):
    first, second, core, way = position()
    count, count_first = outgoing_ref.shape[0], base_ref.shape[1]
    me = first * ways + way

    def place(i):
        return (i // ways, lax.rem(i, ways) * CORES + core)

    def along_first(d):
        to = lax.rem(first + d, count_first)
        return remote(share_ref, base_ref.at[way, first], base_s.at[to], base_r.at[first], (to, second))

    def landed(source):
        return remote(
            share_ref, base_ref.at[way, source], base_s.at[source], base_r.at[source], (source, second)
        )

    def onward(source, k):
        to = lax.rem(way + k, ways)
        return remote(
            base_ref.at[way, source],
            base_ref.at[way, source],
            pass_s.at[to, source],
            pass_r.at[way, source],
            (first, to * CORES + core),
        )

    def handed(source, k):
        giver = lax.rem(way + k, ways)
        return remote(
            base_ref.at[giver, source],
            base_ref.at[giver, source],
            pass_s.at[giver, source],
            pass_r.at[giver, source],
            (first, giver * CORES + core),
        )

    greet(me, count, place)
    pl.semaphore_wait(pltpu.get_barrier_semaphore(), count - 1)
    group = (outgoing_ref, arrived_ref, sends, recvs, me, count, place)

    def begin(d, carry):
        along_first(d).start()
        return carry

    lax.fori_loop(1, count_first, begin, 0)
    exchange_start(*group)
    arrived_ref[me] = outgoing_ref[me]
    base_ref[way, first] = share_ref[...]
    for k in range(1, ways):
        onward(first, k).start()

    def relay(d, carry):
        source = lax.rem(first + count_first - d, count_first)
        landed(source).wait_recv()
        for k in range(1, ways):
            onward(source, k).start()
        return carry

    lax.fori_loop(1, count_first, relay, 0)
    exchange_wait(*group)
    exchange_drain(*group)

    def drain(d, carry):
        along_first(d).wait_send()
        return carry

    lax.fori_loop(1, count_first, drain, 0)

    def end(source, carry):
        for k in range(1, ways):
            handed(source, k).wait_recv()
            onward(source, k).wait_send()
        return carry

    lax.fori_loop(0, count_first, end, 0)


def gather_kernel(mine_ref, other_ref, out_ref, got_ref, mix_ref, swap_s, swap_r, sends, recvs):
    me, second, core, _ = position()
    count = mine_ref.shape[0]
    sibling = (me, second + 1 - 2 * core)

    def place(i):
        return (i, second)

    greet(me, count, place)
    barrier = pltpu.get_barrier_semaphore()
    pl.semaphore_signal(barrier, inc=1, device_id=sibling, device_id_type=pl.DeviceIdType.MESH)
    pl.semaphore_wait(barrier, count)

    def swap(i):
        return remote(other_ref.at[i], got_ref.at[i], swap_s.at[i], swap_r.at[i], sibling)

    def begin(d, carry):
        swap(lax.rem(me + d, count)).start()
        return carry

    lax.fori_loop(1, count + 1, begin, 0)

    def send(d, carry):
        to = lax.rem(me + d, count)
        swap(to).wait_recv()
        mix_ref[to] = mine_ref[to] + got_ref[to]
        remote(mix_ref.at[to], out_ref.at[me], sends.at[to], recvs.at[me], place(to)).start()
        return carry

    lax.fori_loop(1, count, send, 0)
    swap(me).wait_recv()
    out_ref[me] = mine_ref[me] + got_ref[me]
    group = (mix_ref, out_ref, sends, recvs, me, count, place)
    exchange_wait(*group)
    exchange_drain(*group)

    def end(i, carry):
        swap(i).wait_send()
        return carry

    lax.fori_loop(0, count, end, 0)


def scatter_kernel(evolved_ref, mine_ref, other_ref, swap_s, swap_r, sends, recvs):
    me, second, core, _ = position()
    count = evolved_ref.shape[0]
    sibling = (me, second + 1 - 2 * core)

    def place(i):
        return (i, second)

    greet(me, count, place)
    barrier = pltpu.get_barrier_semaphore()
    pl.semaphore_signal(barrier, inc=1, device_id=sibling, device_id_type=pl.DeviceIdType.MESH)
    pl.semaphore_wait(barrier, count)

    def swap(i):
        return remote(mine_ref.at[i], other_ref.at[i], swap_s.at[i], swap_r.at[i], sibling)

    group = (evolved_ref, mine_ref, sends, recvs, me, count, place)
    exchange_start(*group)
    mine_ref[me] = evolved_ref[me]
    swap(me).start()
    exchange_wait(*group, then=lambda source: swap(source).start())
    exchange_drain(*group)

    def end(i, carry):
        swap(i).wait()
        return carry

    lax.fori_loop(0, count, end, 0)


def project_kernel(
    ways, piece, tall, total_rows, order_ref, mine_ref, other_ref, basis_ref, ortho_ref, proj_ref, upper_ref,
    rows_ref, table_ref, leaving_ref, landed_ref, stack_ref, near_ref, far_ref, sends, recvs, near_s, near_r, far_s, far_r,
):
    first, second, core, way = position()
    count = leaving_ref.shape[0]
    count_second, count_first = near_ref.shape[0], far_ref.shape[0]
    vecs = BLK // ways
    me = first * ways + way

    def place(i):
        return (i // ways, lax.rem(i, ways) * CORES + core)

    greet(me, count, place)
    barrier = pltpu.get_barrier_semaphore()
    for k in range(ways):
        pl.semaphore_signal(
            barrier, inc=1, device_id=(first, k * CORES + 1 - core), device_id_type=pl.DeviceIdType.MESH
        )
    pl.semaphore_wait(barrier, count - 1 + ways)
    group = (leaving_ref, landed_ref, sends, recvs, me, count, place)
    padded = leaving_ref.shape[2]
    half = tall // CORES
    step = next(size for size in (48, 40, 32, 16, 8) if piece % size == 0)

    for in_ref, which in ((mine_ref, core), (other_ref, 1 - core)):

        def moment(m, carry):
            for r in range(half):
                start = pl.multiple_of((m * tall + half * which + r) * LANES, LANES)
                block = jnp.concatenate([in_ref[v, m, r : r + 1, :] for v in range(vecs)], 0)
                table_ref[pl.ds(start, LANES), 0:vecs] = block.T
            return carry

        lax.fori_loop(0, 5, moment, 0)

    if padded > piece:
        rows_ref[piece:padded, :] = jnp.zeros((padded - piece, LANES), jnp.float32)

    def collect(i):
        base = (CORES * i + core) * piece

        def rows(j, carry):
            at = pl.multiple_of(j * step, 8)
            held = [table_ref[pl.ds(order_ref[0, base + at + t], 1), :] for t in range(step)]
            for t in range(step):
                rows_ref[pl.ds(at + t, 1), :] = held[t]
            return carry

        lax.fori_loop(0, piece // step, rows, 0)
        for start in range(0, padded, LANES):
            block = rows_ref[start : start + LANES, :].T
            leaving_ref[i, :, start : start + LANES] = block[0:vecs, :]

    def panel(d, carry):
        to = lax.rem(me + d, count)
        collect(to)
        remote(leaving_ref.at[to], landed_ref.at[me], sends.at[to], recvs.at[me], place(to)).start()
        return carry

    lax.fori_loop(1, count, panel, 0)
    collect(me)
    landed_ref[me] = leaving_ref[me]
    stack_ref[0:KB] = basis_ref[...]
    exchange_wait(*group)
    for p in range(count_first):
        for k in range(ways):
            stack_ref[KB + k * vecs : KB + (k + 1) * vecs, p * piece : (p + 1) * piece] = landed_ref[
                p * ways + k, :, 0:piece
            ]
    highest = lax.Precision.HIGHEST
    across = (((1,), (1,)), ((), ()))
    stack = stack_ref[...]
    inner = lax.dot_general(stack, stack, across, precision=highest, preferred_element_type=jnp.float32)

    near_ref[second] = jnp.concatenate([inner[0:32], inner[32:64]], 1)
    group_near = (near_ref, near_ref, near_s, near_r, second, count_second, lambda i: (first, i))
    share(*group_near)
    summed = near_ref[0]
    for i in range(1, count_second):
        summed = summed + near_ref[i]
    far_ref[first] = summed
    group_far = (far_ref, far_ref, far_s, far_r, first, count_first, lambda i: (i, second))
    share(*group_far)
    summed = far_ref[0]
    for i in range(1, count_first):
        summed = summed + far_ref[i]
    summed = summed * (1.0 / total_rows)
    inner = jnp.concatenate([summed[:, 0:64], summed[:, 64:128]], 0)
    proj = inner[0:KB, KB:]
    proj_ref[...] = proj
    mixed = inner[KB:, 0:KB]
    twice = 2.0 * proj - jnp.dot(inner[0:KB, 0:KB], proj, precision=highest, preferred_element_type=jnp.float32)
    gram = inner[KB:, KB:] - jnp.dot(mixed, twice, precision=highest, preferred_element_type=jnp.float32)

    row_at = lax.broadcasted_iota(jnp.int32, (BLK, LANES), 0)
    lane_at = lax.broadcasted_iota(jnp.int32, (BLK, LANES), 1)
    unit = jnp.where(row_at == lane_at, 1.0, 0.0)
    left = jnp.concatenate(
        [gram, -mixed, unit[:, 0:BLK], jnp.zeros((BLK, LANES - 2 * BLK - KB), jnp.float32)], 1
    )
    solved = jnp.zeros((BLK, LANES), jnp.float32)
    for j in range(BLK):
        pivot = jnp.sqrt(left[j : j + 1, j : j + 1])
        row = left[j : j + 1, :] / pivot
        column = left[:, j : j + 1] / pivot
        solved = jnp.where(row_at == j, row, solved)
        left = left - jnp.where(row_at > j, column * row, 0.0)
    upper_ref[...] = jnp.where(lane_at >= row_at, solved, 0.0)[:, 0:BLK]
    ortho_ref[...] = jnp.dot(
        solved[:, BLK : 2 * BLK + KB], stack_ref[...], precision=highest, preferred_element_type=jnp.float32
    )
    exchange_drain(*group)
    drain_share(*group_near)
    drain_share(*group_far)


def share(held, _, sends, recvs, me, count, place):
    def start(d, carry):
        to = lax.rem(me + d, count)
        remote(held.at[me], held.at[me], sends.at[to], recvs.at[me], place(to)).start()
        return carry

    def wait(d, carry):
        source = lax.rem(me + count - d, count)
        remote(held.at[source], held.at[source], sends.at[source], recvs.at[source], place(source)).wait_recv()
        return carry

    lax.fori_loop(1, count, start, 0)
    lax.fori_loop(1, count, wait, 0)


def drain_share(held, _, sends, recvs, me, count, place):
    def drain(d, carry):
        to = lax.rem(me + d, count)
        remote(held.at[me], held.at[me], sends.at[to], recvs.at[me], place(to)).wait_send()
        return carry

    lax.fori_loop(1, count, drain, 0)


def vmem():
    return pl.BlockSpec(memory_space=pltpu.VMEM)


def smem():
    return pl.BlockSpec(memory_space=pltpu.SMEM)


def params(collective=None):
    if collective is None:
        return pltpu.CompilerParams(vmem_limit_bytes=VMEM_BYTES)
    return pltpu.CompilerParams(
        vmem_limit_bytes=VMEM_BYTES, collective_id=collective, has_side_effects=True
    )


def cost(micros):
    return pl.CostEstimate(flops=0, bytes_accessed=int(micros * 3.6e6), transcendentals=0)


def semaphores(count, pairs):
    return [pltpu.SemaphoreType.DMA((count,))] * (2 * pairs)


def body(basis, velocity, temper, flags, order):
    count_first = lax.axis_size("bxy")
    count_second = lax.axis_size("bz")
    devices = count_first * count_second
    panel_rows = basis.shape[1]
    piece = panel_rows // count_first
    slab_rows = piece * devices
    total_rows = panel_rows * devices
    tall, third = temper.shape[1:]
    ways = count_second // CORES
    vecs = BLK // ways
    parts = count_first // vecs
    high = tall // CORES // parts
    wide = -(-(tall // CORES + 4) // 8) * 8
    piece_wide = -(-(high + 4) // 8) * 8
    padded = -(-piece // LANES) * LANES
    panels = devices // CORES
    me_first = lax.axis_index("bxy")
    core = lax.rem(lax.axis_index("bz"), CORES)

    height = lax.broadcasted_iota(jnp.int32, temper.shape, 1)
    solid = (flags == 1) | (height == 0) | (height == tall - 1)
    base = jnp.concatenate([velocity, temper[None], solid.astype(jnp.float32)[None]], 0)
    base = base.transpose(1, 0, 2, 3)
    ring = jnp.concatenate([base[:, :, tall - 2 :], base, base[:, :, : wide]], 2)
    way = lax.axis_index("bz") // CORES
    rows = wide // ways
    ring = lax.dynamic_slice_in_dim(ring, core * (tall // CORES) + way * rows, rows, 2)[0]

    outgoing = basis[KB - BLK :].reshape(ways, vecs, count_first, piece).transpose(2, 0, 1, 3)
    outgoing = jnp.pad(outgoing, ((0, 0), (0, 0), (0, 0), (0, padded - piece)))
    outgoing = outgoing.reshape(panels, vecs, padded)
    arrived, ring = pl.pallas_call(
        functools.partial(panels_kernel, ways),
        out_shape=(
            jax.ShapeDtypeStruct((panels, vecs, padded), jnp.float32),
            jax.ShapeDtypeStruct((ways, count_first, 5, rows, third), jnp.float32),
        ),
        in_specs=[vmem(), vmem()],
        out_specs=(vmem(), vmem()),
        scratch_shapes=semaphores(panels, 1)
        + semaphores(count_first, 1)
        + [pltpu.SemaphoreType.DMA((ways, count_first))] * 2,
        compiler_params=params(0),
        cost_estimate=cost(18),
    )(outgoing, ring)
    part_shape = jax.ShapeDtypeStruct((vecs, 5, wide, third), jnp.float32)
    mine, other = pl.pallas_call(
        functools.partial(spread_kernel, piece, tall),
        out_shape=(part_shape, part_shape),
        in_specs=[smem(), vmem()],
        out_specs=(vmem(), vmem()),
        scratch_shapes=[
            pltpu.VMEM((padded, LANES), jnp.float32),
            pltpu.VMEM((slab_rows, LANES), jnp.float32),
        ],
        compiler_params=params(),
        cost_estimate=cost(28),
    )(order, arrived)
    part = me_first // vecs
    if parts > 1:
        ring = ring.transpose(1, 2, 0, 3, 4).reshape(count_first, 5, wide, third)
        ring = lax.dynamic_slice_in_dim(ring, part * high, piece_wide, 2)[None]
        mine, other = [
            jnp.concatenate([array[:, :, s * high : s * high + piece_wide] for s in range(parts)], 0)
            for array in (mine, other)
        ]
    block = (count_first, 5, piece_wide, third)
    fields = pl.pallas_call(
        gather_kernel,
        out_shape=jax.ShapeDtypeStruct(block, jnp.float32),
        in_specs=[vmem(), vmem()],
        out_specs=vmem(),
        scratch_shapes=[pltpu.VMEM(block, jnp.float32)] * 2 + semaphores(count_first, 2),
        compiler_params=params(1),
        cost_estimate=cost(12),
    )(mine, other)

    state = pltpu.VMEM((26, count_first, piece_wide, third), jnp.float32)
    evolved = pl.pallas_call(
        functools.partial(lattice_kernel, count_first, high),
        out_shape=jax.ShapeDtypeStruct((count_first, 5, high, third), jnp.float32),
        in_specs=[vmem(), vmem()],
        out_specs=vmem(),
        scratch_shapes=[state, state],
        compiler_params=params(),
    )(fields, ring)

    half_shape = jax.ShapeDtypeStruct((count_first, 5, high, third), jnp.float32)
    back, back_other = pl.pallas_call(
        scatter_kernel,
        out_shape=(half_shape, half_shape),
        in_specs=[vmem()],
        out_specs=(vmem(), vmem()),
        scratch_shapes=semaphores(count_first, 2),
        compiler_params=params(2),
        cost_estimate=cost(12),
    )(evolved)
    if parts > 1:
        back, back_other = [
            array.reshape(parts, vecs, 5, high, third)
            .transpose(1, 2, 0, 3, 4)
            .reshape(vecs, 5, parts * high, third)
            for array in (back, back_other)
        ]
    return pl.pallas_call(
        functools.partial(project_kernel, ways, piece, tall, total_rows),
        out_shape=(
            jax.ShapeDtypeStruct((BLK, panel_rows), jnp.float32),
            jax.ShapeDtypeStruct((KB, BLK), jnp.float32),
            jax.ShapeDtypeStruct((BLK, BLK), jnp.float32),
        ),
        in_specs=[smem(), vmem(), vmem(), vmem()],
        out_specs=(vmem(), vmem(), vmem()),
        scratch_shapes=[
            pltpu.VMEM((padded, LANES), jnp.float32),
            pltpu.VMEM((slab_rows, LANES), jnp.float32),
            pltpu.VMEM((panels, vecs, padded), jnp.float32),
            pltpu.VMEM((panels, vecs, padded), jnp.float32),
            pltpu.VMEM((KB + BLK, panel_rows), jnp.float32),
            pltpu.VMEM((count_second, 32, LANES), jnp.float32),
            pltpu.VMEM((count_first, 32, LANES), jnp.float32),
        ]
        + semaphores(panels, 1)
        + semaphores(count_second, 1)
        + semaphores(count_first, 1),
        compiler_params=params(3),
        cost_estimate=cost(50),
    )(order, back, back_other, basis)


def solution(mesh):
    in_specs = (
        P(None, ("bxy", "bz")),
        P(None, "bxy", None, None),
        P("bxy", None, None),
        P("bxy", None, None),
        P("bxy", None),
    )
    out_specs = (P(None, ("bxy", "bz")), P(), P())
    return jax.shard_map(body, mesh=mesh, in_specs=in_specs, out_specs=out_specs, check_vma=False)
```
